256 devices in a mesh: seq: 32 (over x, y, core), tp: 8 (over z).
Axes of the slice: x: 4, y: 4, z: 8, core: 2. Of those that a mesh axis runs over, the one named last changes fastest.
Arguments:
- x_in: bfloat16 [16384, 8192], P('seq', 'tp'), may hold values from -6 to 6
- b_in: bfloat16 [16384, 1024], P('seq', 'tp'), may hold values from -6 to 6
- c_in: bfloat16 [16384, 1024], P('seq', 'tp'), may hold values from -6 to 6
- z_in: bfloat16 [16384, 8192], P('seq', 'tp'), may hold values from -6 to 6
- step_size: float32 [16384, 128], P('seq', 'tp'), may hold values from 0 to 0.4
- log_decay: float32 [16384, 128], P('seq', 'tp'), may hold values from -0.7 to 0
- conv_x: float32 [4, 8192], P(None, 'tp'), may hold values from -3 to 3
- conv_b: float32 [4, 1024], P(None, 'tp'), may hold values from -3 to 3
- conv_c: float32 [4, 1024], P(None, 'tp'), may hold values from -3 to 3
- d_skip: float32 [128], P('tp'), may hold values from 0.5 to 2
- norm_gain: float32 [8192], P('tp'), may hold values from 0.1 to 1.9
- out_weight: bfloat16 [8192, 4096], P('tp'), may hold values from -127 to 127, as said below
- out_exponent: int32 [4096], replicated, may hold values from -14 to -12
- out_sign: int32 [4096], replicated, may hold values from -1 to 1, as said below
Outputs:
- layer_out: bfloat16 [16384, 4096], P(('seq', 'tp'))
The draws below stay inside these ranges and needn't reach their ends.
Inputs may be any that keep to these rules, and one draw needn't show every extreme that they name: `out_weight`: every entry is an integer. `out_sign`: every entry is -1 or 1.
All inputs are finite; a program needn't handle non-finite values.
Results may differ from the reference program's by a relative error of at most 0.0053.
Values may be sent and summed in bfloat16 or wider, within the bound.
No kernel may reach another device: no remote copies, remote signals or barrier semaphores. Data moves between devices by JAX's collectives and lax.ppermute only.
A program may use at most 128 MiB of HBM per device.

```python
import math
import jax
import jax.numpy as jnp
from jax import lax

D = 4096
HEADS = 128
HEAD_DIM = 64
STATE = 128
GROUPS = 8
CONV = 4
SPAN = 256
HAD_BLOCK = 128
TOK_DEV = 512
TOKENS = 16384
INNER = 8192


def head_speed(key):
    return jax.random.uniform(key, (HEADS,), jnp.float32)


def log_uniform(key, shape, lower, upper):
    return jnp.exp(jax.random.uniform(key, shape, jnp.float32, math.log(lower), math.log(upper)))


def draw_log_decay(key, part):
    speeds = head_speed(key)
    key = jax.random.fold_in(key, 11)
    keys = jax.random.split(key, 6)
    share = 0.5
    quick = speeds < share
    quick_rate = 1.0 / jax.random.uniform(keys[0], (HEADS,), jnp.float32, 30.0, 50.0)
    slow_rate = log_uniform(keys[1], (HEADS,), 0.03, 0.12) / TOKENS
    base = jnp.where(quick, quick_rate, slow_rate)
    rough = log_uniform(keys[2], (TOKENS, HEADS), 0.5, 2.0)
    blocks = log_uniform(keys[3], (TOKENS // TOK_DEV, HEADS), 0.5, 2.0)
    block_factor = jnp.repeat(blocks, TOK_DEV, axis=0)
    spots = jax.random.randint(keys[4], (3,), 0, TOKENS)
    struck = jnp.any(jnp.arange(TOKENS)[:, None] == spots[None, :], axis=1)
    loss = jax.random.uniform(keys[5], (TOKENS, HEADS), jnp.float32, 0.22, 0.51)
    return -(base[None, :] * rough * block_factor + jnp.where(struck[:, None], loss, 0.0))


def draw_step_size(key, part):
    speeds = head_speed(key)
    key = jax.random.fold_in(key, 12)
    keys = jax.random.split(key, 3)
    share = 0.5
    quick = speeds < share
    quick_step = log_uniform(keys[0], (HEADS,), 0.05, 0.2)
    slow_step = log_uniform(keys[1], (HEADS,), 2.0, 8.0) / TOKENS
    base = jnp.where(quick, quick_step, slow_step)
    rough = log_uniform(keys[2], (TOKENS, HEADS), 0.5, 2.0)
    return base[None, :] * rough


def draw_out_weight(key, part):
    key = jax.random.fold_in(key, 13)
    levels = jax.random.randint(key, (INNER, D), -127, 128)
    return levels.astype(jnp.float32).astype(jnp.bfloat16)


def draw_out_sign(key, part):
    key = jax.random.fold_in(key, 14)
    return jax.random.randint(key, (D,), 0, 2) * 2 - 1


def place_ends(array, own_key, low, high):
    longest = array.shape.index(max(array.shape))
    spots = []
    for shift in (0, 1):
        where = [jax.random.randint(jax.random.fold_in(own_key, axis), (), 0, length) for axis, length in enumerate(array.shape)]
        where[longest] = (where[longest] + shift) % array.shape[longest]
        spots.append(tuple(where))
    return array.at[spots[0]].set(low).at[spots[1]].set(high)


def block_levels(own_key, shape, cuts, smallest, high):
    def one(dim, shards_of):
        steps = jax.random.uniform(jax.random.fold_in(jax.random.fold_in(own_key, 6), dim), (shards_of,), jnp.float32, smallest / len(cuts), high / len(cuts))
        return jnp.repeat(jnp.exp(steps), shape[dim] // shards_of).reshape((-1,) + (1,) * (len(shape) - dim - 1))

    level = one(*cuts[0])
    for cut in cuts[1:]:
        level = level * one(*cut)
    return level


def bell_draw(own_key, extent, scale, most, cuts=(), held_as=jnp.bfloat16):
    values = jax.random.normal(own_key, extent, jnp.float32) * scale
    if len(cuts) > 0:
        values = block_levels(own_key, extent, cuts, -0.22, 0.18) * values
    return jnp.clip(values, min=-most, max=most).astype(held_as)


def setup_inputs(seed: int = 0) -> dict:
    splits = jax.random.split(jax.random.key(seed), 15)
    return {
        "x_in": bell_draw(splits[0], (TOKENS, INNER), 1.0, 6.0, ((0, 32), (1, 8))),
        "b_in": bell_draw(splits[1], (TOKENS, GROUPS * STATE), 1.0, 6.0, ((0, 32), (1, 8))),
        "c_in": bell_draw(splits[2], (TOKENS, GROUPS * STATE), 1.0, 6.0, ((0, 32), (1, 8))),
        "z_in": bell_draw(splits[3], (TOKENS, INNER), 1.0, 6.0, ((0, 32), (1, 8))),
        "step_size": draw_step_size(jax.random.fold_in(splits[14], 71), 0),
        "log_decay": draw_log_decay(jax.random.fold_in(splits[14], 71), 0),
        "conv_x": bell_draw(splits[6], (CONV, INNER), CONV ** -0.5, 3.0, ((1, 8),), jnp.float32),
        "conv_b": bell_draw(splits[7], (CONV, GROUPS * STATE), CONV ** -0.5, 3.0, ((1, 8),), jnp.float32),
        "conv_c": bell_draw(splits[8], (CONV, GROUPS * STATE), CONV ** -0.5, 3.0, ((1, 8),), jnp.float32),
        "d_skip": jnp.clip(jnp.exp(math.log(2.0) - 1.3862944 * jax.random.uniform(splits[9], (HEADS,), jnp.float32) ** block_levels(splits[9], (HEADS,), ((0, 8),), -0.2, 0.2)), 0.5, 2.0),
        "norm_gain": jnp.clip(1.0 + 0.18 * jax.random.normal(splits[10], (INNER,), jnp.float32), 0.1, 1.9),
        "out_weight": draw_out_weight(jax.random.fold_in(splits[14], 71), 0),
        "out_exponent": place_ends(jax.random.randint(splits[12], (D,), -14, -11), jax.random.fold_in(splits[12], 1), -14, (-11) - 1).astype(jnp.int32),
        "out_sign": draw_out_sign(jax.random.fold_in(splits[14], 71), 0),
    }


HIGHEST = lax.Precision.HIGHEST

def sylvester(order):
    index = jnp.arange(order)
    matrix = jnp.ones((order, order), jnp.float32)
    bit = 1
    while bit < order:
        upper = index // bit % 2
        matrix = matrix * (1.0 - 2.0 * (upper[:, None] * upper[None, :]).astype(jnp.float32))
        bit = bit * 2
    return matrix

def causal_conv(values, kernel, rim):
    padded = jnp.concatenate([rim, values], 0).astype(jnp.float32)
    length = values.shape[0]
    total = kernel[0][None, :] * padded[0:length]
    for offset in range(1, kernel.shape[0]):
        total = total + kernel[offset][None, :] * padded[offset:offset + length]
    return jax.nn.silu(total).astype(jnp.bfloat16)

def span_scan(inputs, keys_b, reads_c, steps, decays, skip, start_state):
    length, heads, width = inputs.shape
    groups = keys_b.shape[1]
    per_group = heads // groups
    blocks_count = length // SPAN
    order = jnp.arange(SPAN)
    lower = (order[:, None] >= order[None, :])[:, :, None]

    def advance(state, block):
        values, enter, leave, step_block, decay_block = block
        running = jnp.cumsum(decay_block, axis=0)
        spread = running[:, None, :] - running[None, :, :]
        mixing = jnp.where(lower, jnp.exp(jnp.where(lower, spread, 0.0)), 0.0)
        scores = jnp.einsum('tgn,sgn->tsg', leave, enter, preferred_element_type=jnp.float32)
        scores = jnp.repeat(scores, per_group, axis=2)
        weights = (mixing * scores * step_block[None, :, :]).astype(jnp.bfloat16)
        inside = jnp.einsum('tsh,shp->thp', weights, values, preferred_element_type=jnp.float32)
        leave_heads = jnp.repeat(leave, per_group, axis=1)
        enter_heads = jnp.repeat(enter, per_group, axis=1)
        start_read = state.astype(jnp.bfloat16)
        carried = jnp.exp(running)[:, :, None] * jnp.einsum('thn,hpn->thp', leave_heads, start_read, preferred_element_type=jnp.float32)
        output = inside + carried + skip[None, :, None] * values.astype(jnp.float32)
        toward_end = jnp.exp(running[-1][None, :] - running) * step_block
        feed = (values.astype(jnp.float32) * toward_end[:, :, None]).astype(jnp.bfloat16)
        new_state = jnp.exp(running[-1])[:, None, None] * state + jnp.einsum('shp,shn->hpn', feed, enter_heads, preferred_element_type=jnp.float32)
        return (new_state, output)
    blocks = tuple((item.reshape((blocks_count, SPAN) + item.shape[1:]) for item in (inputs, keys_b, reads_c, steps, decays)))
    end_state, outputs = lax.scan(advance, start_state, blocks)
    return (outputs.reshape(length, heads, width), end_state)

def gate_norm(flat, gate, gain, group_width):
    gated = flat * jax.nn.silu(gate.astype(jnp.float32))
    grouped = gated.reshape(gated.shape[0], -1, group_width)
    meansq = lax.optimization_barrier(jnp.mean(grouped * grouped, axis=2, keepdims=True))
    normed = (grouped * lax.rsqrt(meansq + 1e-05)).reshape(gated.shape) * gain[None, :]
    return normed.astype(jnp.bfloat16)

def rotate(values, table):
    count, width = values.shape
    blocked = values.reshape(count, width // table.shape[0], table.shape[0])
    return jnp.einsum('rbk,kj->rbj', blocked, table, precision=HIGHEST).reshape(count, width)

def reference(x_in, b_in, c_in, z_in, step_size, log_decay, conv_x, conv_b, conv_c, d_skip, norm_gain, out_weight, out_exponent, out_sign):
    joined = jnp.concatenate([x_in, b_in, c_in], 1)
    kernel = jnp.concatenate([conv_x, conv_b, conv_c], 1)
    rim = jnp.zeros((CONV - 1, joined.shape[1]), jnp.bfloat16)
    mixed = causal_conv(joined, kernel, rim)
    band = GROUPS * STATE
    inputs = mixed[:, :INNER].reshape(TOKENS, HEADS, HEAD_DIM)
    keys_b = mixed[:, INNER:INNER + band].reshape(TOKENS, GROUPS, STATE)
    reads_c = mixed[:, INNER + band:].reshape(TOKENS, GROUPS, STATE)
    start_state = jnp.zeros((HEADS, HEAD_DIM, STATE), jnp.float32)
    outputs, ignored = span_scan(inputs, keys_b, reads_c, step_size, log_decay, d_skip, start_state)
    normed = gate_norm(outputs.reshape(TOKENS, INNER), z_in, norm_gain, INNER // GROUPS)
    weight_wide = out_weight.astype(jnp.float32)
    column_scale = jnp.exp2(out_exponent.astype(jnp.float32)) * out_sign.astype(jnp.float32)
    table = sylvester(HAD_BLOCK) / jnp.float32(math.sqrt(HAD_BLOCK))

    def finish(block):
        summed = jnp.dot(block.astype(jnp.float32), weight_wide, precision=HIGHEST)
        return rotate(summed * column_scale[None, :], table.astype(jnp.float32)).astype(jnp.bfloat16)
    blocks = normed.reshape(TOKENS // TOK_DEV, TOK_DEV, INNER)
    return lax.map(finish, blocks).reshape(TOKENS, D)
```

```python
import math

import jax
import jax.numpy as jnp
from jax import lax
from jax.experimental import pallas as pl
from jax.experimental.pallas import tpu as pltpu
from jax.sharding import PartitionSpec as P

HEAD_DIM = 64
STATE = 128
SPAN = 256
HAD_BLOCK = 128
HEADS_LOCAL = 16
TOK = 512
CH = 1024
PARTS = 32
PIECE = 32
PAY = 48
TILE = 256
MIB = 1024 * 1024

F32 = jnp.float32
BF16 = jnp.bfloat16
HIGHEST = lax.Precision.HIGHEST


def dot(a, b, dims=((1,), (0,)), precision=None):
    return lax.dot_general(a, b, (dims, ((), ())), precision=precision, preferred_element_type=F32)


def conv_silu(pad, rim, values, taps):
    width = values.shape[1]
    pad[0:8, 0:width] = rim[8:16].astype(F32)
    pad[8 : TOK + 8, 0:width] = values.astype(F32)
    total = taps[0:1] * pad[5 : 5 + TOK, 0:width]
    for k in range(1, 4):
        total = total + taps[k : k + 1] * pad[5 + k : 5 + k + TOK, 0:width]
    return jax.nn.silu(total).astype(BF16)


def head_rows(first, channels):
    head = lax.broadcasted_iota(jnp.int32, (HEADS_LOCAL, channels), 0)
    channel = lax.broadcasted_iota(jnp.int32, (HEADS_LOCAL, channels), 1)
    return (channel // HEAD_DIM + first == head).astype(F32)


def head_columns(first, channels, row):
    channel = lax.broadcasted_iota(jnp.int32, (channels, HEADS_LOCAL), 0)
    head = lax.broadcasted_iota(jnp.int32, (channels, HEADS_LOCAL), 1)
    return jnp.sum(jnp.where(channel // HEAD_DIM + first == head, row, 0.0), axis=1, keepdims=True)


def scan_in(rim_x, rim_b, rim_c, x, b, c, step, decay, tap_x, tap_b, tap_c,
            xs_o, bs_o, cs_o, run_o, pay_o, first_o, pad, toward):
    tile = pl.program_id(0)

    @pl.when(tile == 0)
    def _():
        bs_o[...] = conv_silu(pad, rim_b[...], b[...], tap_b[...])
        cs_o[...] = conv_silu(pad, rim_c[...], c[...], tap_c[...])
        later = lax.broadcasted_iota(jnp.int32, (SPAN, SPAN), 0)
        earlier = lax.broadcasted_iota(jnp.int32, (SPAN, SPAN), 1)
        lower = (later >= earlier).astype(F32)
        for k in range(2):
            rows = slice(k * SPAN, (k + 1) * SPAN)
            running = dot(lower, decay[rows], precision=HIGHEST)
            run_o[rows] = running
            toward[rows] = jnp.exp(running[SPAN - 1 :] - running) * step[rows]

    xs = conv_silu(pad, rim_x[...], x[...], tap_x[...])
    xs_o[...] = xs
    first = tile * (TILE // HEAD_DIM)
    wide = dot(toward[...], head_rows(first, TILE), precision=HIGHEST)
    feed = (xs.astype(F32) * wide).astype(BF16)
    one = dot(feed[:SPAN], bs_o[:SPAN], ((0,), (0,)))
    two = dot(feed[SPAN:], bs_o[SPAN:], ((0,), (0,)))
    first_o[...] = one
    end0 = run_o[SPAN - 1 : SPAN]
    end1 = run_o[TOK - 1 : TOK]
    state = jnp.exp(head_columns(first, TILE, end1)) * one + two
    pay_o[:, 0:PIECE, :] = state.astype(BF16).reshape(TILE // PIECE, PIECE, STATE)
    total = jnp.broadcast_to(head_columns(first, TILE, end0 + end1), (TILE, STATE))
    high = total.astype(BF16)
    rest = total - high.astype(F32)
    middle = rest.astype(BF16)
    low = (rest - middle.astype(F32)).astype(BF16)
    row = lax.broadcasted_iota(jnp.int32, (TILE, STATE), 0) % PIECE
    parts = jnp.where(row == 0, high.astype(F32), jnp.where(row == 1, middle.astype(F32), low.astype(F32)))
    pay_o[:, PIECE:PAY, :] = parts.astype(BF16).reshape(TILE // PIECE, PIECE, STATE)[:, 0 : PAY - PIECE, :]


def prefix(got, out):
    state = jnp.zeros((PIECE, STATE), F32)
    for k in range(PARTS):
        out[k] = state.astype(BF16)
        if k < PARTS - 1:
            piece = got[k].astype(F32)
            total = piece[PIECE : PIECE + 1] + piece[PIECE + 1 : PIECE + 2] + piece[PIECE + 2 : PIECE + 3]
            state = jnp.exp(total) * state + piece[:PIECE]


def inside(xs, bs, cs, run, decay, step, skip, out, scores, run_t, step_t):
    tile = pl.program_id(0)

    @pl.when(tile == 0)
    def _():
        later = lax.broadcasted_iota(jnp.int32, (SPAN, SPAN), 0)
        earlier = lax.broadcasted_iota(jnp.int32, (SPAN, SPAN), 1)
        upper = (later <= earlier).astype(F32)
        same = (later == earlier).astype(F32)
        for k in range(2):
            rows = slice(k * SPAN, (k + 1) * SPAN)
            raw = dot(cs[rows], bs[rows], ((1,), (1,)))
            scores[rows] = jnp.where(later >= earlier, raw, 0.0)
            run_t[:, rows] = dot(decay[rows], upper, ((0,), (0,)), precision=HIGHEST)
            step_t[:, rows] = dot(step[rows], same, ((0,), (0,)), precision=HIGHEST)

    per_tile = TILE // HEAD_DIM
    head_lane = lax.broadcasted_iota(jnp.int32, (HEADS_LOCAL, 1), 0)
    lane_head = lax.broadcasted_iota(jnp.int32, (TOK, HEADS_LOCAL), 1)
    for q in range(per_tile):
        head = tile * per_tile + q
        column = jnp.sum(jnp.where(lane_head == head, run[...], 0.0), axis=1, keepdims=True)
        r_row = jnp.sum(jnp.where(head_lane == head, run_t[...], 0.0), axis=0, keepdims=True)
        s_row = jnp.sum(jnp.where(head_lane == head, step_t[...], 0.0), axis=0, keepdims=True)
        lanes = slice(q * HEAD_DIM, (q + 1) * HEAD_DIM)
        for k in range(2):
            rows = slice(k * SPAN, (k + 1) * SPAN)
            spread = jnp.minimum(column[rows] - r_row[:, rows], 0.0)
            weights = (jnp.exp(spread) * scores[rows] * s_row[:, rows]).astype(BF16)
            out[rows, lanes] = dot(weights, xs[rows, lanes])
    out[...] = out[...] + skip[...] * xs[...].astype(F32)


def norm_project(y, cs, run, first, incoming, z, gain, weight, normed_o, part_o):
    @pl.when(pl.program_id(0) == 0)
    def _():
        end0 = run[SPAN - 1 : SPAN]
        expand = head_rows(0, CH)
        for k in range(2):
            rows = slice(k * SPAN, (k + 1) * SPAN)
            if k == 0:
                start = incoming[...]
            else:
                start = (jnp.exp(head_columns(0, CH, end0)) * incoming[...].astype(F32) + first[...]).astype(BF16)
            grown = dot(jnp.exp(run[rows]), expand, precision=HIGHEST)
            carried = grown * dot(cs[rows], start, ((1,), (1,)))
            gated = (y[rows] + carried) * jax.nn.silu(z[rows].astype(F32))
            meansq = jnp.sum(gated * gated, axis=1, keepdims=True) * (1.0 / CH)
            normed_o[rows] = (gated * lax.rsqrt(meansq + 1e-05) * gain[...]).astype(BF16)

    part_o[...] = dot(normed_o[...], weight[...])


def project(normed, weight, part_o):
    part_o[...] = dot(normed[...], weight[...])


def finish(own, up, down, scale, out):
    total = (own[...] + up[...].astype(F32) + down[...].astype(F32)) * scale[...]
    high = total.astype(BF16)
    rest = total - high.astype(F32)
    middle = rest.astype(BF16)
    low = (rest - middle.astype(F32)).astype(BF16)
    row = lax.broadcasted_iota(jnp.int32, (HAD_BLOCK, HAD_BLOCK), 0)
    column = lax.broadcasted_iota(jnp.int32, (HAD_BLOCK, HAD_BLOCK), 1)
    ones = row & column
    parity = jnp.zeros_like(ones)
    for bit in range(7):
        parity = parity ^ ((ones >> bit) & 1)
    table = (1 - 2 * parity).astype(F32).astype(BF16)
    for k in range(total.shape[1] // HAD_BLOCK):
        lanes = slice(k * HAD_BLOCK, (k + 1) * HAD_BLOCK)
        rotated = dot(high[:, lanes], table) + dot(middle[:, lanes], table) + dot(low[:, lanes], table)
        out[:, lanes] = (rotated * (1.0 / math.sqrt(HAD_BLOCK))).astype(BF16)


def whole(shape):
    return pl.BlockSpec(shape, lambda i: (0,) * len(shape))


def tiled(shape, axis):
    return pl.BlockSpec(shape, lambda i: tuple(i if d == axis else 0 for d in range(len(shape))))


def params(mib):
    return pltpu.CompilerParams(vmem_limit_bytes=mib * MIB)


def ring(value, step):
    count = lax.axis_size("tp")
    return lax.ppermute(value, "tp", [(k, (k + step) % count) for k in range(count)])


def local(x_in, b_in, c_in, z_in, step_size, log_decay, conv_x, conv_b, conv_c, d_skip, norm_gain,
          out_weight, out_exponent, out_sign):
    seq = lax.axis_size("seq")
    tail = jnp.concatenate([x_in[TOK - 16 :], b_in[TOK - 16 :], c_in[TOK - 16 :]], 1)
    rim = lax.ppermute(tail, "seq", [(k, k + 1) for k in range(seq - 1)])
    tiles = CH // TILE
    xs, bs, cs, run, pay, first = pl.pallas_call(
        scan_in,
        grid=(tiles,),
        in_specs=[
            tiled((16, TILE), 1),
            pl.BlockSpec((16, STATE), lambda i: (0, CH // STATE)),
            pl.BlockSpec((16, STATE), lambda i: (0, CH // STATE + 1)),
            tiled((TOK, TILE), 1),
            whole((TOK, STATE)),
            whole((TOK, STATE)),
            whole((TOK, HEADS_LOCAL)),
            whole((TOK, HEADS_LOCAL)),
            tiled((4, TILE), 1),
            whole((4, STATE)),
            whole((4, STATE)),
        ],
        out_specs=[
            tiled((TOK, TILE), 1),
            whole((TOK, STATE)),
            whole((TOK, STATE)),
            whole((TOK, HEADS_LOCAL)),
            tiled((TILE // PIECE, PAY, STATE), 0),
            tiled((TILE, STATE), 0),
        ],
        out_shape=[
            jax.ShapeDtypeStruct((TOK, CH), BF16),
            jax.ShapeDtypeStruct((TOK, STATE), BF16),
            jax.ShapeDtypeStruct((TOK, STATE), BF16),
            jax.ShapeDtypeStruct((TOK, HEADS_LOCAL), F32),
            jax.ShapeDtypeStruct((PARTS, PAY, STATE), BF16),
            jax.ShapeDtypeStruct((CH, STATE), F32),
        ],
        scratch_shapes=[pltpu.VMEM((TOK + 8, TILE), F32), pltpu.VMEM((TOK, HEADS_LOCAL), F32)],
        compiler_params=params(32),
        cost_estimate=pl.CostEstimate(flops=10**9, bytes_accessed=4 * 10**6, transcendentals=10**6),
        name="scan_in",
    )(rim, rim, rim, x_in, b_in, c_in, step_size, log_decay, conv_x, conv_b, conv_c)

    got = lax.all_to_all(pay, "seq", 0, 0, tiled=True)
    y = pl.pallas_call(
        inside,
        grid=(tiles,),
        in_specs=[
            tiled((TOK, TILE), 1),
            whole((TOK, STATE)),
            whole((TOK, STATE)),
            whole((TOK, HEADS_LOCAL)),
            whole((TOK, HEADS_LOCAL)),
            whole((TOK, HEADS_LOCAL)),
            tiled((1, TILE), 1),
        ],
        out_specs=tiled((TOK, TILE), 1),
        out_shape=jax.ShapeDtypeStruct((TOK, CH), F32),
        scratch_shapes=[
            pltpu.VMEM((TOK, SPAN), F32),
            pltpu.VMEM((HEADS_LOCAL, TOK), F32),
            pltpu.VMEM((HEADS_LOCAL, TOK), F32),
        ],
        compiler_params=params(32),
        cost_estimate=pl.CostEstimate(flops=4 * 10**9, bytes_accessed=6 * 10**6, transcendentals=2 * 10**6),
        name="inside",
    )(xs, bs, cs, run, log_decay, step_size, jnp.repeat(d_skip, HEAD_DIM)[None, :])

    before = pl.pallas_call(
        prefix,
        out_shape=jax.ShapeDtypeStruct((PARTS, PIECE, STATE), BF16),
        name="prefix",
    )(got)
    incoming = lax.all_to_all(before, "seq", 0, 0, tiled=True).reshape(CH, STATE)

    model = out_weight.shape[1]
    half = model // 2
    step_cols = 512
    normed, part_a = pl.pallas_call(
        norm_project,
        grid=(half // step_cols,),
        in_specs=[
            whole((TOK, CH)),
            whole((TOK, STATE)),
            whole((TOK, HEADS_LOCAL)),
            whole((CH, STATE)),
            whole((CH, STATE)),
            whole((TOK, CH)),
            whole((1, CH)),
            tiled((CH, step_cols), 1),
        ],
        out_specs=[whole((TOK, CH)), tiled((TOK, step_cols), 1)],
        out_shape=[jax.ShapeDtypeStruct((TOK, CH), BF16), jax.ShapeDtypeStruct((TOK, half), F32)],
        compiler_params=params(40),
        name="norm_project",
    )(y, cs, run, first, incoming, z_in, norm_gain[None, :], out_weight)
    part_b = pl.pallas_call(
        project,
        grid=(half // step_cols,),
        in_specs=[
            whole((TOK, CH)),
            pl.BlockSpec((CH, step_cols), lambda i: (0, i + half // step_cols)),
        ],
        out_specs=tiled((TOK, step_cols), 1),
        out_shape=jax.ShapeDtypeStruct((TOK, half), F32),
        compiler_params=params(32),
        cost_estimate=pl.CostEstimate(flops=2 * 10**9, bytes_accessed=8 * 10**6, transcendentals=0),
        name="project",
    )(normed, out_weight)

    place = lax.axis_index("tp")
    count = lax.axis_size("tp")
    share = TOK // count
    scale = jnp.exp2(out_exponent.astype(F32)) * out_sign.astype(F32)
    results = []
    for group, part in enumerate((part_a, part_b)):

        def mine(distance, part=part):
            row = lax.rem(place + distance + count, count) * share
            return lax.dynamic_slice_in_dim(part, row, share, 0)

        ends = []
        up = count // 2 if group == 0 else count // 2 - 1
        for sign, hops in ((1, up), (-1, count - 1 - up)):
            value = mine(sign * hops).astype(BF16)
            for k in range(hops - 1, -1, -1):
                value = ring(value, sign)
                if k > 0:
                    value = (value.astype(F32) + mine(sign * k)).astype(BF16)
            ends.append(value)
        results.append(
            pl.pallas_call(
                finish,
                out_shape=jax.ShapeDtypeStruct((share, half), BF16),
                name="finish",
            )(mine(0), ends[0], ends[1], scale[None, group * half : (group + 1) * half])
        )
    return jnp.concatenate(results, 1)


def solution(mesh):
    return jax.shard_map(
        local,
        mesh=mesh,
        in_specs=(
            P("seq", "tp"),
            P("seq", "tp"),
            P("seq", "tp"),
            P("seq", "tp"),
            P("seq", "tp"),
            P("seq", "tp"),
            P(None, "tp"),
            P(None, "tp"),
            P(None, "tp"),
            P("tp"),
            P("tp"),
            P("tp", None),
            P(),
            P(),
        ),
        out_specs=P(("seq", "tp"), None),
        check_vma=False,
    )
```

```python
import math

import jax
import jax.numpy as jnp
from jax import lax
from jax.experimental import pallas as pl
from jax.experimental.pallas import tpu as pltpu
from jax.sharding import PartitionSpec as P

HEAD_DIM = 64
STATE = 128
SPAN = 256
HAD_BLOCK = 128
HEADS_LOCAL = 16
TOK = 512
CH = 1024
PARTS = 32
PIECE = 32
PAY = 48
TILE = 256
ROWS = 128
SHARE = 64
MIB = 1024 * 1024
LIMIT = dict(tail_rows=58, scan_in=58, scan_edge=58, inside=58, prefix=16, norm_first=52, project=58, ring=50)

F32 = jnp.float32
BF16 = jnp.bfloat16
HIGHEST = lax.Precision.HIGHEST


def dot(a, b, dims=((1,), (0,)), precision=None):
    return lax.dot_general(a, b, (dims, ((), ())), precision=precision, preferred_element_type=F32)


def conv_silu(pad, rim, values, taps):
    width = values.shape[1]
    pad[0:8, 0:width] = rim[8:16].astype(F32)
    pad[8 : TOK + 8, 0:width] = values.astype(F32)
    total = taps[0:1] * pad[5 : 5 + TOK, 0:width]
    for k in range(1, 4):
        total = total + taps[k : k + 1] * pad[5 + k : 5 + k + TOK, 0:width]
    return jax.nn.silu(total).astype(BF16)


def head_rows(first, channels):
    head = lax.broadcasted_iota(jnp.int32, (HEADS_LOCAL, channels), 0)
    channel = lax.broadcasted_iota(jnp.int32, (HEADS_LOCAL, channels), 1)
    return (channel // HEAD_DIM + first == head).astype(F32)


def head_columns(first, channels, row):
    channel = lax.broadcasted_iota(jnp.int32, (channels, HEADS_LOCAL), 0)
    head = lax.broadcasted_iota(jnp.int32, (channels, HEADS_LOCAL), 1)
    return jnp.sum(jnp.where(channel // HEAD_DIM + first == head, row, 0.0), axis=1, keepdims=True)


def tail_rows(x, b, c, out):
    out[:, 0:CH] = x[...]
    out[:, CH : CH + STATE] = b[...]
    out[:, CH + STATE :] = c[...]


def scan_in(x, b, c, step_t, decay_t, tap_x, tap_b, tap_c, xs_o, bs_o, cs_o, run_o, toward_o, one_o, two_o, pad):
    tile = pl.program_id(0)

    @pl.when(tile == 0)
    def _():
        empty = jnp.zeros((16, STATE), BF16)
        bs_o[...] = conv_silu(pad, empty, b[...], tap_b[...])
        cs_o[...] = conv_silu(pad, empty, c[...], tap_c[...])
        later = lax.broadcasted_iota(jnp.int32, (SPAN, SPAN), 0)
        earlier = lax.broadcasted_iota(jnp.int32, (SPAN, SPAN), 1)
        lower = (later >= earlier).astype(F32)
        same = (later == earlier).astype(F32)
        for k in range(2):
            rows = slice(k * SPAN, (k + 1) * SPAN)
            running = dot(lower, decay_t[:, rows], ((1,), (1,)), precision=HIGHEST)
            step = dot(same, step_t[:, rows], ((1,), (1,)), precision=HIGHEST)
            run_o[rows] = running
            toward_o[rows] = jnp.exp(running[SPAN - 1 :] - running) * step

    xs = conv_silu(pad, jnp.zeros((16, TILE), BF16), x[...], tap_x[...])
    xs_o[...] = xs
    first = tile * (TILE // HEAD_DIM)
    wide = dot(toward_o[...], head_rows(first, TILE), precision=HIGHEST)
    row = lax.broadcasted_iota(jnp.int32, (TOK, 1), 0)
    feed = jnp.where(row < 8, 0.0, xs.astype(F32) * wide).astype(BF16)
    one_o[...] = dot(feed[:SPAN], bs_o[:SPAN], ((0,), (0,)))
    two_o[...] = dot(feed[SPAN:], bs_o[SPAN:], ((0,), (0,)))


def conv_head(rim, values, taps):
    padded = jnp.concatenate([rim.astype(F32), values.astype(F32)], 0)
    total = taps[0:1] * padded[13:29]
    for k in range(1, 4):
        total = total + taps[k : k + 1] * padded[13 + k : 29 + k]
    return jax.nn.silu(total).astype(BF16)


def scan_edge(rim, x, b, c, tap_x, tap_b, tap_c, toward, run0, run1, one, two, xs_in, bs_in, cs_in,
              xs_o, bs_o, cs_o, first_o, pay_o):
    xs = conv_head(rim[:, 0:CH], x[...], tap_x[...])
    bs = conv_head(rim[:, CH : CH + STATE], b[...], tap_b[...])
    xs_o[...] = xs
    bs_o[...] = bs
    cs_o[...] = conv_head(rim[:, CH + STATE :], c[...], tap_c[...])
    wide = dot(toward[...], head_rows(0, CH), precision=HIGHEST)
    row = lax.broadcasted_iota(jnp.int32, (16, 1), 0)
    feed = jnp.where(row < 8, xs.astype(F32) * wide, 0.0).astype(BF16)
    first = one[...] + dot(feed, bs, ((0,), (0,)))
    first_o[...] = first
    end0 = run0[7:8]
    end1 = run1[7:8]
    state = jnp.exp(head_columns(0, CH, end1)) * first + two[...]
    pay_o[:, 0:PIECE, :] = state.astype(BF16).reshape(PARTS, PIECE, STATE)
    total = head_columns(0, CH, end0 + end1).reshape(PARTS, PIECE, 1)[:, 0 : PAY - PIECE, :]
    total = jnp.broadcast_to(total, (PARTS, PAY - PIECE, STATE))
    high = total.astype(BF16).astype(F32)
    rest = total - high
    middle = rest.astype(BF16).astype(F32)
    low = rest - middle
    row = lax.broadcasted_iota(jnp.int32, total.shape, 1)
    pay_o[:, PIECE:PAY, :] = jnp.where(row == 0, high, jnp.where(row == 1, middle, low)).astype(BF16)


def prefix(got, out):
    log_total = got[:, PIECE : PIECE + 8, :].astype(F32)
    grow = jnp.exp(log_total[:, 0:1] + log_total[:, 1:2] + log_total[:, 2:3])
    state = jnp.zeros((PIECE, STATE), F32)
    for k in range(PARTS):
        out[k] = state.astype(BF16)
        if k < PARTS - 1:
            state = grow[k] * state + got[k, 0:PIECE, :].astype(F32)


def inside(xs, bs, cs, run, decay_t, step_t, skip, z, y_o, grow_o, scores, run_t):
    tile = pl.program_id(0)

    @pl.when(tile == 0)
    def _():
        later = lax.broadcasted_iota(jnp.int32, (SPAN, SPAN), 0)
        earlier = lax.broadcasted_iota(jnp.int32, (SPAN, SPAN), 1)
        upper = (later <= earlier).astype(F32)
        for k in range(2):
            rows = slice(k * SPAN, (k + 1) * SPAN)
            raw = dot(cs[rows], bs[rows], ((1,), (1,)))
            scores[rows] = jnp.where(later >= earlier, raw, 0.0)
            run_t[:, rows] = dot(decay_t[:, rows], upper, precision=HIGHEST)

    per_tile = TILE // HEAD_DIM
    head_lane = lax.broadcasted_iota(jnp.int32, (HEADS_LOCAL, 1), 0)
    lane_head = lax.broadcasted_iota(jnp.int32, (TOK, HEADS_LOCAL), 1)
    for q in range(per_tile):
        head = tile * per_tile + q
        column = jnp.sum(jnp.where(lane_head == head, run[...], 0.0), axis=1, keepdims=True)
        r_row = jnp.sum(jnp.where(head_lane == head, run_t[...], 0.0), axis=0, keepdims=True)
        s_row = jnp.sum(jnp.where(head_lane == head, step_t[...], 0.0), axis=0, keepdims=True)
        lanes = slice(q * HEAD_DIM, (q + 1) * HEAD_DIM)
        for k in range(2):
            rows = slice(k * SPAN, (k + 1) * SPAN)
            spread = jnp.minimum(column[rows] - r_row[:, rows], 0.0)
            weights = (jnp.exp(spread) * scores[rows] * s_row[:, rows]).astype(BF16)
            y_o[rows, lanes] = dot(weights, xs[rows, lanes])
    gate = jax.nn.silu(z[...].astype(F32))
    y_o[...] = (y_o[...] + skip[...] * xs[...].astype(F32)) * gate
    grow_o[...] = dot(jnp.exp(run[...]), head_rows(tile * per_tile, TILE), precision=HIGHEST) * gate


def norm_first(y, grow, cs, run, first, incoming, gain, weight, normed_o, up_o, down_o, start, held, picked, sem):
    step = pl.program_id(0)
    fetch = pltpu.make_async_copy(weight.at[:, 0 : held.shape[1]], held, sem)

    @pl.when(step == 0)
    def _():
        fetch.start()
        start[...] = incoming[...]

    @pl.when(step == SPAN // ROWS)
    def _():
        decay = jnp.exp(head_columns(0, CH, run[7:8]))
        start[...] = (decay * incoming[...].astype(F32) + first[...]).astype(BF16)

    carried = dot(cs[...], start[...], ((1,), (1,)))
    gated = y[...] + grow[...] * carried
    meansq = jnp.sum(gated * gated, axis=1, keepdims=True) * (1.0 / CH)
    rows = pl.ds(pl.multiple_of(step * ROWS, ROWS), ROWS)
    normed_o[rows] = (gated * lax.rsqrt(meansq + 1e-05) * gain[...]).astype(BF16)

    @pl.when(step == TOK // ROWS - 1)
    def _():
        place = lax.axis_index("tp")
        for k, distance in enumerate((4, 5)):
            at = pl.multiple_of(lax.rem(place + distance, 8) * SHARE, SHARE)
            picked[k * SHARE : (k + 1) * SHARE] = normed_o[pl.ds(at, SHARE)]
        fetch.wait()
        for k in range(held.shape[1] // 512):
            lanes = slice(k * 512, (k + 1) * 512)
            both = dot(picked[...], held[:, lanes]).astype(BF16)
            up_o[:, lanes] = both[:SHARE]
            down_o[:, lanes] = both[SHARE:]


def project(normed, weight, part_o):
    part_o[...] = dot(normed[...], weight[...])


def add_hop(place, came, part, out):
    out[...] = (came[...].astype(F32) + part[...]).astype(BF16)


def first_hop(place, part_up, part_down, up_o, down_o):
    up_o[...] = part_up[...].astype(BF16)
    down_o[...] = part_down[...].astype(BF16)


def finish(place, own, up_a, down_a, up_b, down_b, scale, out):
    row = lax.broadcasted_iota(jnp.int32, (HAD_BLOCK, HAD_BLOCK), 0)
    column = lax.broadcasted_iota(jnp.int32, (HAD_BLOCK, HAD_BLOCK), 1)
    ones = row & column
    ones = ones ^ (ones >> 4)
    ones = ones ^ (ones >> 2)
    ones = ones ^ (ones >> 1)
    table = (1 - 2 * (ones & 1)).astype(F32).astype(BF16)
    half = up_a.shape[1]
    for group, (up, down) in enumerate(((up_a, down_a), (up_b, down_b))):
        at = slice(group * half, (group + 1) * half)
        total = (own[:, at] + up[...].astype(F32) + down[...].astype(F32)) * scale[:, at]
        stacked = jnp.concatenate(
            [total[:, k * HAD_BLOCK : (k + 1) * HAD_BLOCK] for k in range(half // HAD_BLOCK)], 0
        )
        high = stacked.astype(BF16)
        rest = stacked - high.astype(F32)
        middle = rest.astype(BF16)
        low = (rest - middle.astype(F32)).astype(BF16)
        rotated = dot(high, table) + dot(middle, table) + dot(low, table)
        rotated = (rotated * (1.0 / math.sqrt(HAD_BLOCK))).astype(BF16)
        for k in range(half // HAD_BLOCK):
            lanes = slice(group * half + k * HAD_BLOCK, group * half + (k + 1) * HAD_BLOCK)
            out[:, lanes] = rotated[k * SHARE : (k + 1) * SHARE]


def whole(shape):
    return pl.BlockSpec(shape, lambda i: (0,) * len(shape))


def tiled(shape, axis):
    return pl.BlockSpec(shape, lambda i: tuple(i if d == axis else 0 for d in range(len(shape))))


def params(mib):
    return pltpu.CompilerParams(vmem_limit_bytes=mib * MIB)


def ring(value, step):
    count = lax.axis_size("tp")
    return lax.ppermute(value, "tp", [(k, (k + step) % count) for k in range(count)])


def shape(dims, dtype):
    return jax.ShapeDtypeStruct(dims, dtype)


def block(dims, *index):
    return pl.BlockSpec(dims, lambda i: index)


def local(x_in, b_in, c_in, z_in, step_size, log_decay, conv_x, conv_b, conv_c, d_skip, norm_gain,
          out_weight, out_exponent, out_sign):
    seq = lax.axis_size("seq")
    tiles = CH // TILE
    step_t = step_size.T
    decay_t = log_decay.T
    last = TOK // 16 - 1
    tail = pl.pallas_call(
        tail_rows,
        grid=(1,),
        in_specs=[block((16, CH), last, 0), block((16, STATE), last, 0), block((16, STATE), last, 0)],
        out_specs=whole((16, CH + 2 * STATE)),
        out_shape=shape((16, CH + 2 * STATE), BF16),
        compiler_params=params(LIMIT["tail_rows"]),
        name="tail_rows",
    )(x_in, b_in, c_in)
    rim = lax.ppermute(tail, "seq", [(k, k + 1) for k in range(seq - 1)])
    xs, bs, cs, run, toward, one, two = pl.pallas_call(
        scan_in,
        grid=(tiles,),
        in_specs=[
            tiled((TOK, TILE), 1),
            whole((TOK, STATE)),
            whole((TOK, STATE)),
            whole((HEADS_LOCAL, TOK)),
            whole((HEADS_LOCAL, TOK)),
            tiled((4, TILE), 1),
            whole((4, STATE)),
            whole((4, STATE)),
        ],
        out_specs=[
            tiled((TOK, TILE), 1),
            whole((TOK, STATE)),
            whole((TOK, STATE)),
            whole((TOK, HEADS_LOCAL)),
            whole((TOK, HEADS_LOCAL)),
            tiled((TILE, STATE), 0),
            tiled((TILE, STATE), 0),
        ],
        out_shape=[
            shape((TOK, CH), BF16),
            shape((TOK, STATE), BF16),
            shape((TOK, STATE), BF16),
            shape((TOK, HEADS_LOCAL), F32),
            shape((TOK, HEADS_LOCAL), F32),
            shape((CH, STATE), F32),
            shape((CH, STATE), F32),
        ],
        scratch_shapes=[pltpu.VMEM((TOK + 8, TILE), F32)],
        compiler_params=params(LIMIT["scan_in"]),
        cost_estimate=pl.CostEstimate(flops=10**9, bytes_accessed=4 * 10**6, transcendentals=10**6),
        name="scan_in",
    )(x_in, b_in, c_in, step_t, decay_t, conv_x, conv_b, conv_c)

    xs, bs, cs, first, pay = pl.pallas_call(
        scan_edge,
        grid=(1,),
        in_specs=[
            whole((16, CH + 2 * STATE)),
            whole((16, CH)),
            whole((16, STATE)),
            whole((16, STATE)),
            whole((4, CH)),
            whole((4, STATE)),
            whole((4, STATE)),
            whole((16, HEADS_LOCAL)),
            block((8, HEADS_LOCAL), SPAN // 8 - 1, 0),
            block((8, HEADS_LOCAL), TOK // 8 - 1, 0),
            whole((CH, STATE)),
            whole((CH, STATE)),
            pl.BlockSpec(memory_space=pl.ANY),
            pl.BlockSpec(memory_space=pl.ANY),
            pl.BlockSpec(memory_space=pl.ANY),
        ],
        out_specs=[
            whole((16, CH)),
            whole((16, STATE)),
            whole((16, STATE)),
            whole((CH, STATE)),
            whole((PARTS, PAY, STATE)),
        ],
        out_shape=[
            shape((TOK, CH), BF16),
            shape((TOK, STATE), BF16),
            shape((TOK, STATE), BF16),
            shape((CH, STATE), F32),
            shape((PARTS, PAY, STATE), BF16),
        ],
        input_output_aliases={12: 0, 13: 1, 14: 2},
        compiler_params=params(LIMIT["scan_edge"]),
        name="scan_edge",
    )(rim, x_in, b_in, c_in, conv_x, conv_b, conv_c, toward, run, run, one, two, xs, bs, cs)

    got = lax.all_to_all(pay, "seq", 0, 0, tiled=True)
    y, grow = pl.pallas_call(
        inside,
        grid=(tiles,),
        in_specs=[
            tiled((TOK, TILE), 1),
            whole((TOK, STATE)),
            whole((TOK, STATE)),
            whole((TOK, HEADS_LOCAL)),
            whole((HEADS_LOCAL, TOK)),
            whole((HEADS_LOCAL, TOK)),
            tiled((1, TILE), 1),
            tiled((TOK, TILE), 1),
        ],
        out_specs=[tiled((TOK, TILE), 1), tiled((TOK, TILE), 1)],
        out_shape=[shape((TOK, CH), F32), shape((TOK, CH), F32)],
        scratch_shapes=[pltpu.VMEM((TOK, SPAN), F32), pltpu.VMEM((HEADS_LOCAL, TOK), F32)],
        compiler_params=params(LIMIT["inside"]),
        cost_estimate=pl.CostEstimate(flops=4 * 10**9, bytes_accessed=6 * 10**6, transcendentals=2 * 10**6),
        name="inside",
    )(xs, bs, cs, run, decay_t, step_t, jnp.repeat(d_skip, HEAD_DIM)[None, :], z_in)

    before = pl.pallas_call(
        prefix,
        grid=(1,),
        in_specs=[whole((PARTS, PAY, STATE))],
        out_specs=whole((PARTS, PIECE, STATE)),
        out_shape=shape((PARTS, PIECE, STATE), BF16),
        compiler_params=params(LIMIT["prefix"]),
        name="prefix",
    )(got)
    incoming = lax.all_to_all(before, "seq", 0, 0, tiled=True).reshape(CH, STATE)

    model = out_weight.shape[1]
    half = model // 2
    step_cols = 512
    normed, up_a, down_a = pl.pallas_call(
        norm_first,
        grid=(TOK // ROWS,),
        in_specs=[
            tiled((ROWS, CH), 0),
            tiled((ROWS, CH), 0),
            tiled((ROWS, STATE), 0),
            block((8, HEADS_LOCAL), SPAN // 8 - 1, 0),
            whole((CH, STATE)),
            whole((CH, STATE)),
            whole((1, CH)),
            pl.BlockSpec(memory_space=pl.ANY),
        ],
        out_specs=[whole((TOK, CH)), whole((SHARE, half)), whole((SHARE, half))],
        out_shape=[shape((TOK, CH), BF16), shape((SHARE, half), BF16), shape((SHARE, half), BF16)],
        scratch_shapes=[
            pltpu.VMEM((CH, STATE), BF16),
            pltpu.VMEM((CH, half), BF16),
            pltpu.VMEM((2 * SHARE, CH), BF16),
            pltpu.SemaphoreType.DMA,
        ],
        compiler_params=params(LIMIT["norm_first"]),
        name="norm_first",
    )(y, grow, cs, run, first, incoming, norm_gain[None, :], out_weight)
    part = pl.pallas_call(
        project,
        grid=(model // step_cols,),
        in_specs=[whole((TOK, CH)), tiled((CH, step_cols), 1)],
        out_specs=tiled((TOK, step_cols), 1),
        out_shape=shape((TOK, model), F32),
        compiler_params=params(LIMIT["project"]),
        cost_estimate=pl.CostEstimate(flops=2 * 10**10, bytes_accessed=16 * 10**6, transcendentals=0),
        name="project",
    )(normed, out_weight)

    count = lax.axis_size("tp")
    place = lax.axis_index("tp").astype(jnp.int32)[None]
    scale = jnp.exp2(out_exponent.astype(F32)) * out_sign.astype(F32)

    def chunk(distance, group):
        return pl.BlockSpec((SHARE, half), lambda i, at: (lax.rem(at[0] + distance + count, count), group))

    message = pl.BlockSpec((SHARE, half), lambda i, at: (0, 0))

    def call(kernel, in_specs, outs, out_specs, *operands):
        return pl.pallas_call(
            kernel,
            grid_spec=pltpu.PrefetchScalarGridSpec(
                num_scalar_prefetch=1, grid=(1,), in_specs=in_specs, out_specs=out_specs
            ),
            out_shape=outs,
            compiler_params=params(LIMIT["ring"]),
            cost_estimate=pl.CostEstimate(flops=10**6, bytes_accessed=10**6, transcendentals=0),
            name=kernel.__name__,
        )(place, *operands)

    sent = shape((SHARE, half), BF16)
    up_b, down_b = call(first_hop, [chunk(3, 1), chunk(-4, 1)], [sent, sent], [message, message], part, part)
    ends = []
    for group, up in enumerate((count // 2, count // 2 - 1)):
        starts = (up_a, down_a) if group == 0 else (up_b, down_b)
        for value, sign, hops in ((starts[0], 1, up), (starts[1], -1, count - 1 - up)):
            for k in range(hops - 1, -1, -1):
                value = ring(value, sign)
                if k > 0:
                    value = call(add_hop, [message, chunk(sign * k, group)], sent, message, value, part)
            ends.append(value)
    return call(
        finish,
        [pl.BlockSpec((SHARE, model), lambda i, at: (at[0], 0))]
        + [message] * 4
        + [pl.BlockSpec((1, model), lambda i, at: (0, 0))],
        shape((SHARE, model), BF16),
        pl.BlockSpec((SHARE, model), lambda i, at: (0, 0)),
        part,
        *ends,
        scale[None, :],
    )


def solution(mesh):
    return jax.shard_map(
        local,
        mesh=mesh,
        in_specs=(
            P("seq", "tp"),
            P("seq", "tp"),
            P("seq", "tp"),
            P("seq", "tp"),
            P("seq", "tp"),
            P("seq", "tp"),
            P(None, "tp"),
            P(None, "tp"),
            P(None, "tp"),
            P("tp"),
            P("tp"),
            P("tp", None),
            P(),
            P(),
        ),
        out_specs=P(("seq", "tp"), None),
        check_vma=False,
    )
```

```python
import functools
import math

import jax
import jax.numpy as jnp
from jax import lax
from jax.experimental import pallas as pl
from jax.experimental.pallas import tpu as pltpu
from jax.sharding import PartitionSpec as P

HEAD_DIM = 64
STATE = 128
SPAN = 256
HAD_BLOCK = 128
HEADS_LOCAL = 16
TOK = 512
CH = 1024
PARTS = 32
PIECE = 32
PAY = 48
TILE = 256
ROWS = 128
SHARE = 64
BEFORE = 3
MIB = 1024 * 1024
LIMIT = dict(tail_rows=58, scan_in=58, scan_edge=58, inside=58, prefix=16, norm_first=50, project=50, ring=50)

F32 = jnp.float32
BF16 = jnp.bfloat16
HIGHEST = lax.Precision.HIGHEST


def dot(a, b, dims=((1,), (0,)), precision=None):
    return lax.dot_general(a, b, (dims, ((), ())), precision=precision, preferred_element_type=F32)


def conv_silu(pad, rim, values, taps):
    width = values.shape[1]
    pad[0:8, 0:width] = rim[8:16].astype(F32)
    pad[8 : TOK + 8, 0:width] = values.astype(F32)
    total = taps[0:1] * pad[5 : 5 + TOK, 0:width]
    for k in range(1, 4):
        total = total + taps[k : k + 1] * pad[5 + k : 5 + k + TOK, 0:width]
    return jax.nn.silu(total).astype(BF16)


def head_rows(first, channels):
    head = lax.broadcasted_iota(jnp.int32, (HEADS_LOCAL, channels), 0)
    channel = lax.broadcasted_iota(jnp.int32, (HEADS_LOCAL, channels), 1)
    return (channel // HEAD_DIM + first == head).astype(F32)


def head_columns(first, channels, row):
    channel = lax.broadcasted_iota(jnp.int32, (channels, HEADS_LOCAL), 0)
    head = lax.broadcasted_iota(jnp.int32, (channels, HEADS_LOCAL), 1)
    return jnp.sum(jnp.where(channel // HEAD_DIM + first == head, row, 0.0), axis=1, keepdims=True)


def tail_rows(x, b, c, out):
    out[:, 0:CH] = x[...]
    out[:, CH : CH + STATE] = b[...]
    out[:, CH + STATE :] = c[...]


def scan_in(x, b, c, step_t, decay_t, tap_x, tap_b, tap_c, xs_o, bs_o, cs_o, run_o, toward_o, one_o, two_o, pad):
    tile = pl.program_id(0)

    @pl.when(tile == 0)
    def _():
        empty = jnp.zeros((16, STATE), BF16)
        bs_o[...] = conv_silu(pad, empty, b[...], tap_b[...])
        cs_o[...] = conv_silu(pad, empty, c[...], tap_c[...])
        later = lax.broadcasted_iota(jnp.int32, (SPAN, SPAN), 0)
        earlier = lax.broadcasted_iota(jnp.int32, (SPAN, SPAN), 1)
        lower = (later >= earlier).astype(F32)
        same = (later == earlier).astype(F32)
        for k in range(2):
            rows = slice(k * SPAN, (k + 1) * SPAN)
            running = dot(lower, decay_t[:, rows], ((1,), (1,)), precision=HIGHEST)
            step = dot(same, step_t[:, rows], ((1,), (1,)), precision=HIGHEST)
            run_o[rows] = running
            toward_o[rows] = jnp.exp(running[SPAN - 1 :] - running) * step

    xs = conv_silu(pad, jnp.zeros((16, TILE), BF16), x[...], tap_x[...])
    xs_o[...] = xs
    first = tile * (TILE // HEAD_DIM)
    wide = dot(toward_o[...], head_rows(first, TILE), precision=HIGHEST)
    row = lax.broadcasted_iota(jnp.int32, (TOK, 1), 0)
    feed = jnp.where(row < 8, 0.0, xs.astype(F32) * wide).astype(BF16)
    one_o[...] = dot(feed[:SPAN], bs_o[:SPAN], ((0,), (0,)))
    two_o[...] = dot(feed[SPAN:], bs_o[SPAN:], ((0,), (0,)))


def conv_head(rim, values, taps):
    padded = jnp.concatenate([rim.astype(F32), values.astype(F32)], 0)
    total = taps[0:1] * padded[13:29]
    for k in range(1, 4):
        total = total + taps[k : k + 1] * padded[13 + k : 29 + k]
    return jax.nn.silu(total).astype(BF16)


def scan_edge(rim, x, b, c, tap_x, tap_b, tap_c, toward, run0, run1, one, two, xs_in, bs_in, cs_in,
              xs_o, bs_o, cs_o, first_o, pay_o):
    xs = conv_head(rim[:, 0:CH], x[...], tap_x[...])
    bs = conv_head(rim[:, CH : CH + STATE], b[...], tap_b[...])
    xs_o[...] = xs
    bs_o[...] = bs
    cs_o[...] = conv_head(rim[:, CH + STATE :], c[...], tap_c[...])
    wide = dot(toward[...], head_rows(0, CH), precision=HIGHEST)
    row = lax.broadcasted_iota(jnp.int32, (16, 1), 0)
    feed = jnp.where(row < 8, xs.astype(F32) * wide, 0.0).astype(BF16)
    first = one[...] + dot(feed, bs, ((0,), (0,)))
    first_o[...] = first
    end0 = run0[7:8]
    end1 = run1[7:8]
    state = jnp.exp(head_columns(0, CH, end1)) * first + two[...]
    pay_o[:, 0:PIECE, :] = state.astype(BF16).reshape(PARTS, PIECE, STATE)
    total = head_columns(0, CH, end0 + end1).reshape(PARTS, PIECE, 1)[:, 0 : PAY - PIECE, :]
    total = jnp.broadcast_to(total, (PARTS, PAY - PIECE, STATE))
    high = total.astype(BF16).astype(F32)
    rest = total - high
    middle = rest.astype(BF16).astype(F32)
    low = rest - middle
    row = lax.broadcasted_iota(jnp.int32, total.shape, 1)
    pay_o[:, PIECE:PAY, :] = jnp.where(row == 0, high, jnp.where(row == 1, middle, low)).astype(BF16)


def prefix(got, out):
    log_total = got[:, PIECE : PIECE + 8, :].astype(F32)
    grow = jnp.exp(log_total[:, 0:1] + log_total[:, 1:2] + log_total[:, 2:3])
    state = jnp.zeros((PIECE, STATE), F32)
    for k in range(PARTS):
        out[k] = state.astype(BF16)
        if k < PARTS - 1:
            state = grow[k] * state + got[k, 0:PIECE, :].astype(F32)


def inside(xs, bs, cs, run, decay_t, step_t, skip, z, y_o, grow_o, scores, run_t):
    tile = pl.program_id(0)

    @pl.when(tile == 0)
    def _():
        later = lax.broadcasted_iota(jnp.int32, (SPAN, SPAN), 0)
        earlier = lax.broadcasted_iota(jnp.int32, (SPAN, SPAN), 1)
        upper = (later <= earlier).astype(F32)
        for k in range(2):
            rows = slice(k * SPAN, (k + 1) * SPAN)
            raw = dot(cs[rows], bs[rows], ((1,), (1,)))
            scores[rows] = jnp.where(later >= earlier, raw, 0.0)
            run_t[:, rows] = dot(decay_t[:, rows], upper, precision=HIGHEST)

    per_tile = TILE // HEAD_DIM
    head_lane = lax.broadcasted_iota(jnp.int32, (HEADS_LOCAL, 1), 0)
    lane_head = lax.broadcasted_iota(jnp.int32, (TOK, HEADS_LOCAL), 1)
    for q in range(per_tile):
        head = tile * per_tile + q
        column = jnp.sum(jnp.where(lane_head == head, run[...], 0.0), axis=1, keepdims=True)
        r_row = jnp.sum(jnp.where(head_lane == head, run_t[...], 0.0), axis=0, keepdims=True)
        s_row = jnp.sum(jnp.where(head_lane == head, step_t[...], 0.0), axis=0, keepdims=True)
        lanes = slice(q * HEAD_DIM, (q + 1) * HEAD_DIM)
        for k in range(2):
            rows = slice(k * SPAN, (k + 1) * SPAN)
            spread = jnp.minimum(column[rows] - r_row[:, rows], 0.0)
            weights = (jnp.exp(spread) * scores[rows] * s_row[:, rows]).astype(BF16)
            y_o[rows, lanes] = dot(weights, xs[rows, lanes])
    gate = jax.nn.silu(z[...].astype(F32))
    y_o[...] = (y_o[...] + skip[...] * xs[...].astype(F32)) * gate
    grow_o[...] = dot(jnp.exp(run[...]), head_rows(tile * per_tile, TILE), precision=HIGHEST) * gate


def norm_first(y, grow, cs, run, first, incoming, gain, weight, normed_o, up_o, down_o, start, held, picked, sem):
    step = pl.program_id(0)
    fetch = pltpu.make_async_copy(weight.at[:, 0 : held.shape[1]], held, sem)

    @pl.when(step == 0)
    def _():
        fetch.start()
        start[...] = incoming[...]

    @pl.when(step == SPAN // ROWS)
    def _():
        decay = jnp.exp(head_columns(0, CH, run[7:8]))
        start[...] = (decay * incoming[...].astype(F32) + first[...]).astype(BF16)

    carried = dot(cs[...], start[...], ((1,), (1,)))
    gated = y[...] + grow[...] * carried
    meansq = jnp.sum(gated * gated, axis=1, keepdims=True) * (1.0 / CH)
    normed = (gated * lax.rsqrt(meansq + 1e-05) * gain[...]).astype(BF16)
    place = lax.axis_index("tp")
    for k in range(ROWS // SHARE):
        at = lax.rem(step * (ROWS // SHARE) + k - place + 8 + BEFORE, 8) * SHARE
        normed_o[pl.ds(pl.multiple_of(at, SHARE), SHARE)] = normed[k * SHARE : (k + 1) * SHARE]

    @pl.when(step == TOK // ROWS - 1)
    def _():
        fetch.wait()
        picked[0:SHARE] = normed_o[rolled(4)]
        picked[SHARE:] = normed_o[rolled(-3)]
        for k in range(held.shape[1] // 512):
            lanes = slice(k * 512, (k + 1) * 512)
            both = dot(picked[...], held[:, lanes]).astype(BF16)
            up_o[:, lanes] = both[:SHARE]
            down_o[:, lanes] = both[SHARE:]


def rolled(distance):
    first = (distance + BEFORE) % 8 * SHARE
    return slice(first, first + SHARE)


def project_first(normed, weight, up_o, down_o, picked):
    picked[0:SHARE] = normed[rolled(3)]
    picked[SHARE:] = normed[rolled(-4)]
    both = dot(picked[...], weight[...]).astype(BF16)
    up_o[...] = both[:SHARE]
    down_o[...] = both[SHARE:]


def project_rest(lowest, normed, weight, *outs):
    first = rolled(lowest).start
    sums = dot(normed[first : first + len(outs) * SHARE], weight[...])
    for k, out in enumerate(outs):
        out[...] = sums[k * SHARE : (k + 1) * SHARE]


def add_one(came, part, out):
    out[...] = (came[...].astype(F32) + part[...]).astype(BF16)


def add_two(came_up, came_down, part_up, part_down, up_o, down_o):
    up_o[...] = (came_up[...].astype(F32) + part_up[...]).astype(BF16)
    down_o[...] = (came_down[...].astype(F32) + part_down[...]).astype(BF16)


def finish(own_a, own_b, up_a, down_a, up_b, down_b, scale, out):
    row = lax.broadcasted_iota(jnp.int32, (HAD_BLOCK, HAD_BLOCK), 0)
    column = lax.broadcasted_iota(jnp.int32, (HAD_BLOCK, HAD_BLOCK), 1)
    ones = row & column
    ones = ones ^ (ones >> 4)
    ones = ones ^ (ones >> 2)
    ones = ones ^ (ones >> 1)
    table = (1 - 2 * (ones & 1)).astype(F32).astype(BF16)
    half = up_a.shape[1]
    for group, (own, up, down) in enumerate(((own_a, up_a, down_a), (own_b, up_b, down_b))):
        at = slice(group * half, (group + 1) * half)
        total = (own[...] + up[...].astype(F32) + down[...].astype(F32)) * scale[:, at]
        stacked = jnp.concatenate(
            [total[:, k * HAD_BLOCK : (k + 1) * HAD_BLOCK] for k in range(half // HAD_BLOCK)], 0
        )
        high = stacked.astype(BF16)
        rest = stacked - high.astype(F32)
        middle = rest.astype(BF16)
        low = (rest - middle.astype(F32)).astype(BF16)
        rotated = dot(high, table) + dot(middle, table) + dot(low, table)
        rotated = (rotated * (1.0 / math.sqrt(HAD_BLOCK))).astype(BF16)
        for k in range(half // HAD_BLOCK):
            lanes = slice(group * half + k * HAD_BLOCK, group * half + (k + 1) * HAD_BLOCK)
            out[:, lanes] = rotated[k * SHARE : (k + 1) * SHARE]


def whole(shape):
    return pl.BlockSpec(shape, lambda i: (0,) * len(shape))


def tiled(shape, axis):
    return pl.BlockSpec(shape, lambda i: tuple(i if d == axis else 0 for d in range(len(shape))))


def params(mib):
    return pltpu.CompilerParams(vmem_limit_bytes=mib * MIB)


def ring(value, step):
    count = lax.axis_size("tp")
    return lax.ppermute(value, "tp", [(k, (k + step) % count) for k in range(count)])


def shape(dims, dtype):
    return jax.ShapeDtypeStruct(dims, dtype)


def block(dims, *index):
    return pl.BlockSpec(dims, lambda i: index)


def local(x_in, b_in, c_in, z_in, step_size, log_decay, conv_x, conv_b, conv_c, d_skip, norm_gain,
          out_weight, out_exponent, out_sign):
    seq = lax.axis_size("seq")
    tiles = CH // TILE
    step_t = step_size.T
    decay_t = log_decay.T
    last = TOK // 16 - 1
    tail = pl.pallas_call(
        tail_rows,
        grid=(1,),
        in_specs=[block((16, CH), last, 0), block((16, STATE), last, 0), block((16, STATE), last, 0)],
        out_specs=whole((16, CH + 2 * STATE)),
        out_shape=shape((16, CH + 2 * STATE), BF16),
        compiler_params=params(LIMIT["tail_rows"]),
        name="tail_rows",
    )(x_in, b_in, c_in)
    rim = lax.ppermute(tail, "seq", [(k, k + 1) for k in range(seq - 1)])
    xs, bs, cs, run, toward, one, two = pl.pallas_call(
        scan_in,
        grid=(tiles,),
        in_specs=[
            tiled((TOK, TILE), 1),
            whole((TOK, STATE)),
            whole((TOK, STATE)),
            whole((HEADS_LOCAL, TOK)),
            whole((HEADS_LOCAL, TOK)),
            tiled((4, TILE), 1),
            whole((4, STATE)),
            whole((4, STATE)),
        ],
        out_specs=[
            tiled((TOK, TILE), 1),
            whole((TOK, STATE)),
            whole((TOK, STATE)),
            whole((TOK, HEADS_LOCAL)),
            whole((TOK, HEADS_LOCAL)),
            tiled((TILE, STATE), 0),
            tiled((TILE, STATE), 0),
        ],
        out_shape=[
            shape((TOK, CH), BF16),
            shape((TOK, STATE), BF16),
            shape((TOK, STATE), BF16),
            shape((TOK, HEADS_LOCAL), F32),
            shape((TOK, HEADS_LOCAL), F32),
            shape((CH, STATE), F32),
            shape((CH, STATE), F32),
        ],
        scratch_shapes=[pltpu.VMEM((TOK + 8, TILE), F32)],
        compiler_params=params(LIMIT["scan_in"]),
        cost_estimate=pl.CostEstimate(flops=10**9, bytes_accessed=4 * 10**6, transcendentals=10**6),
        name="scan_in",
    )(x_in, b_in, c_in, step_t, decay_t, conv_x, conv_b, conv_c)

    xs, bs, cs, first, pay = pl.pallas_call(
        scan_edge,
        grid=(1,),
        in_specs=[
            whole((16, CH + 2 * STATE)),
            whole((16, CH)),
            whole((16, STATE)),
            whole((16, STATE)),
            whole((4, CH)),
            whole((4, STATE)),
            whole((4, STATE)),
            whole((16, HEADS_LOCAL)),
            block((8, HEADS_LOCAL), SPAN // 8 - 1, 0),
            block((8, HEADS_LOCAL), TOK // 8 - 1, 0),
            whole((CH, STATE)),
            whole((CH, STATE)),
            pl.BlockSpec(memory_space=pl.ANY),
            pl.BlockSpec(memory_space=pl.ANY),
            pl.BlockSpec(memory_space=pl.ANY),
        ],
        out_specs=[
            whole((16, CH)),
            whole((16, STATE)),
            whole((16, STATE)),
            whole((CH, STATE)),
            whole((PARTS, PAY, STATE)),
        ],
        out_shape=[
            shape((TOK, CH), BF16),
            shape((TOK, STATE), BF16),
            shape((TOK, STATE), BF16),
            shape((CH, STATE), F32),
            shape((PARTS, PAY, STATE), BF16),
        ],
        input_output_aliases={12: 0, 13: 1, 14: 2},
        compiler_params=params(LIMIT["scan_edge"]),
        name="scan_edge",
    )(rim, x_in, b_in, c_in, conv_x, conv_b, conv_c, toward, run, run, one, two, xs, bs, cs)

    got = lax.all_to_all(pay, "seq", 0, 0, tiled=True)
    y, grow = pl.pallas_call(
        inside,
        grid=(tiles,),
        in_specs=[
            tiled((TOK, TILE), 1),
            whole((TOK, STATE)),
            whole((TOK, STATE)),
            whole((TOK, HEADS_LOCAL)),
            whole((HEADS_LOCAL, TOK)),
            whole((HEADS_LOCAL, TOK)),
            tiled((1, TILE), 1),
            tiled((TOK, TILE), 1),
        ],
        out_specs=[tiled((TOK, TILE), 1), tiled((TOK, TILE), 1)],
        out_shape=[shape((TOK, CH), F32), shape((TOK, CH), F32)],
        scratch_shapes=[pltpu.VMEM((TOK, SPAN), F32), pltpu.VMEM((HEADS_LOCAL, TOK), F32)],
        compiler_params=params(LIMIT["inside"]),
        cost_estimate=pl.CostEstimate(flops=4 * 10**9, bytes_accessed=6 * 10**6, transcendentals=2 * 10**6),
        name="inside",
    )(xs, bs, cs, run, decay_t, step_t, jnp.repeat(d_skip, HEAD_DIM)[None, :], z_in)

    got, y, grow = lax.optimization_barrier((got, y, grow))
    before = pl.pallas_call(
        prefix,
        grid=(1,),
        in_specs=[whole((PARTS, PAY, STATE))],
        out_specs=whole((PARTS, PIECE, STATE)),
        out_shape=shape((PARTS, PIECE, STATE), BF16),
        compiler_params=params(LIMIT["prefix"]),
        name="prefix",
    )(got)
    incoming = lax.all_to_all(before, "seq", 0, 0, tiled=True).reshape(CH, STATE)

    model = out_weight.shape[1]
    half = model // 2
    step_cols = 512
    normed, up_a, down_a = pl.pallas_call(
        norm_first,
        grid=(TOK // ROWS,),
        in_specs=[
            tiled((ROWS, CH), 0),
            tiled((ROWS, CH), 0),
            tiled((ROWS, STATE), 0),
            block((8, HEADS_LOCAL), SPAN // 8 - 1, 0),
            whole((CH, STATE)),
            whole((CH, STATE)),
            whole((1, CH)),
            pl.BlockSpec(memory_space=pl.ANY),
        ],
        out_specs=[whole((TOK, CH)), whole((SHARE, half)), whole((SHARE, half))],
        out_shape=[shape((TOK, CH), BF16), shape((SHARE, half), BF16), shape((SHARE, half), BF16)],
        scratch_shapes=[
            pltpu.VMEM((CH, STATE), BF16),
            pltpu.VMEM((CH, half), BF16),
            pltpu.VMEM((2 * SHARE, CH), BF16),
            pltpu.SemaphoreType.DMA,
        ],
        compiler_params=params(LIMIT["norm_first"]),
        name="norm_first",
    )(y, grow, cs, run, first, incoming, norm_gain[None, :], out_weight)
    tiles = half // step_cols
    up_b, down_b = pl.pallas_call(
        project_first,
        grid=(tiles,),
        in_specs=[whole((TOK, CH)), pl.BlockSpec((CH, step_cols), lambda i: (0, i + tiles))],
        out_specs=[tiled((SHARE, step_cols), 1)] * 2,
        out_shape=[shape((SHARE, half), BF16)] * 2,
        scratch_shapes=[pltpu.VMEM((2 * SHARE, CH), BF16)],
        compiler_params=params(LIMIT["project"]),
        cost_estimate=pl.CostEstimate(flops=10, bytes_accessed=10, transcendentals=0),
        name="project_first",
    )(normed, out_weight)
    parts = []
    for group, lowest in enumerate((-2, -3)):
        parts.append(
            pl.pallas_call(
                functools.partial(project_rest, lowest),
                grid=(tiles,),
                in_specs=[
                    whole((TOK, CH)),
                    pl.BlockSpec((CH, step_cols), lambda i, group=group: (0, i + group * tiles)),
                ],
                out_specs=[tiled((SHARE, step_cols), 1)] * 6,
                out_shape=[shape((SHARE, half), F32)] * 6,
                compiler_params=params(LIMIT["project"]),
                cost_estimate=pl.CostEstimate(flops=10, bytes_accessed=10, transcendentals=0),
                name="project_rest",
            )(normed, out_weight)
        )
    scale = jnp.exp2(out_exponent.astype(F32)) * out_sign.astype(F32)

    def add(kernel, *operands):
        sent = shape((SHARE, half), BF16)
        return pl.pallas_call(
            kernel,
            in_specs=[pl.BlockSpec(memory_space=pltpu.VMEM)] * len(operands),
            out_specs=[pl.BlockSpec(memory_space=pltpu.VMEM)] * (len(operands) // 2),
            out_shape=[sent] * (len(operands) // 2),
            compiler_params=params(LIMIT["ring"]),
            cost_estimate=pl.CostEstimate(flops=10**6, bytes_accessed=10**6, transcendentals=0),
            name=kernel.__name__,
        )(*operands)

    ends = []
    for group, (up, down) in enumerate(((up_a, down_a), (up_b, down_b))):
        lowest = (-2, -3)[group]
        mine = {distance: parts[group][distance - lowest] for distance in range(lowest, lowest + 6)}
        for hop in range(2):
            up, down = ring(up, 1), ring(down, -1)
            far = 3 - hop if group == 0 else 2 - hop
            up, down = add(add_two, up, down, mine[far], mine[-(5 - far - 2 * hop)])
        up, down = ring(up, 1), ring(down, -1)
        if group == 0:
            (up,) = add(add_one, up, mine[1])
            up = ring(up, 1)
        else:
            (down,) = add(add_one, down, mine[-1])
            down = ring(down, -1)
        ends += [mine[0], up, down]
    return pl.pallas_call(
        finish,
        in_specs=[pl.BlockSpec(memory_space=pltpu.VMEM)] * 7,
        out_specs=pl.BlockSpec(memory_space=pltpu.VMEM),
        out_shape=shape((SHARE, model), BF16),
        compiler_params=params(LIMIT["ring"]),
        name="finish",
    )(ends[0], ends[3], ends[1], ends[2], ends[4], ends[5], scale[None, :])


def solution(mesh):
    return jax.shard_map(
        local,
        mesh=mesh,
        in_specs=(
            P("seq", "tp"),
            P("seq", "tp"),
            P("seq", "tp"),
            P("seq", "tp"),
            P("seq", "tp"),
            P("seq", "tp"),
            P(None, "tp"),
            P(None, "tp"),
            P(None, "tp"),
            P("tp"),
            P("tp"),
            P("tp", None),
            P(),
            P(),
        ),
        out_specs=P(("seq", "tp"), None),
        check_vma=False,
    )
```

```python
import functools
import math

import jax
import jax.numpy as jnp
from jax import lax
from jax.experimental import pallas as pl
from jax.experimental.pallas import tpu as pltpu
from jax.sharding import PartitionSpec as P

HEAD_DIM = 64
STATE = 128
SPAN = 256
HAD_BLOCK = 128
HEADS_LOCAL = 16
TOK = 512
CH = 1024
PARTS = 32
PIECE = 32
PAY = 48
TILE = 256
ROWS = 128
SHARE = 64
BEFORE = 3
MIB = 1024 * 1024
LIMIT = dict(tail_rows=58, scan_in=58, scan_edge=58, inside=58, prefix=16, norm_project=44, ring=24)
PART = jnp.float32

F32 = jnp.float32
BF16 = jnp.bfloat16
HIGHEST = lax.Precision.HIGHEST


def dot(a, b, dims=((1,), (0,)), precision=None):
    return lax.dot_general(a, b, (dims, ((), ())), precision=precision, preferred_element_type=F32)


def conv_silu(pad, rim, values, taps):
    width = values.shape[1]
    pad[0:8, 0:width] = rim[8:16].astype(F32)
    pad[8 : TOK + 8, 0:width] = values.astype(F32)
    total = taps[0:1] * pad[5 : 5 + TOK, 0:width]
    for k in range(1, 4):
        total = total + taps[k : k + 1] * pad[5 + k : 5 + k + TOK, 0:width]
    return jax.nn.silu(total).astype(BF16)


def head_rows(first, channels):
    head = lax.broadcasted_iota(jnp.int32, (HEADS_LOCAL, channels), 0)
    channel = lax.broadcasted_iota(jnp.int32, (HEADS_LOCAL, channels), 1)
    return (channel // HEAD_DIM + first == head).astype(F32)


def head_columns(first, channels, row):
    channel = lax.broadcasted_iota(jnp.int32, (channels, HEADS_LOCAL), 0)
    head = lax.broadcasted_iota(jnp.int32, (channels, HEADS_LOCAL), 1)
    return jnp.sum(jnp.where(channel // HEAD_DIM + first == head, row, 0.0), axis=1, keepdims=True)


def tail_rows(x, b, c, out):
    out[:, 0:CH] = x[...]
    out[:, CH : CH + STATE] = b[...]
    out[:, CH + STATE :] = c[...]


def scan_in(x, b, c, step_t, decay_t, tap_x, tap_b, tap_c, xs_o, bs_o, cs_o, run_o, toward_o, one_o, two_o, pad):
    tile = pl.program_id(0)

    @pl.when(tile == 0)
    def _():
        empty = jnp.zeros((16, STATE), BF16)
        bs_o[...] = conv_silu(pad, empty, b[...], tap_b[...])
        cs_o[...] = conv_silu(pad, empty, c[...], tap_c[...])
        later = lax.broadcasted_iota(jnp.int32, (SPAN, SPAN), 0)
        earlier = lax.broadcasted_iota(jnp.int32, (SPAN, SPAN), 1)
        lower = (later >= earlier).astype(F32)
        same = (later == earlier).astype(F32)
        for k in range(2):
            rows = slice(k * SPAN, (k + 1) * SPAN)
            running = dot(lower, decay_t[:, rows], ((1,), (1,)), precision=HIGHEST)
            step = dot(same, step_t[:, rows], ((1,), (1,)), precision=HIGHEST)
            run_o[rows] = running
            toward_o[rows] = jnp.exp(running[SPAN - 1 :] - running) * step

    xs = conv_silu(pad, jnp.zeros((16, TILE), BF16), x[...], tap_x[...])
    xs_o[...] = xs
    first = tile * (TILE // HEAD_DIM)
    wide = dot(toward_o[...], head_rows(first, TILE), precision=HIGHEST)
    row = lax.broadcasted_iota(jnp.int32, (TOK, 1), 0)
    feed = jnp.where(row < 8, 0.0, xs.astype(F32) * wide).astype(BF16)
    one_o[...] = dot(feed[:SPAN], bs_o[:SPAN], ((0,), (0,)))
    two_o[...] = dot(feed[SPAN:], bs_o[SPAN:], ((0,), (0,)))


def conv_head(rim, values, taps):
    padded = jnp.concatenate([rim.astype(F32), values.astype(F32)], 0)
    total = taps[0:1] * padded[13:29]
    for k in range(1, 4):
        total = total + taps[k : k + 1] * padded[13 + k : 29 + k]
    return jax.nn.silu(total).astype(BF16)


def scan_edge(rim, x, b, c, tap_x, tap_b, tap_c, toward, run0, run1, one, two, xs_in, bs_in, cs_in,
              xs_o, bs_o, cs_o, first_o, pay_o):
    xs = conv_head(rim[:, 0:CH], x[...], tap_x[...])
    bs = conv_head(rim[:, CH : CH + STATE], b[...], tap_b[...])
    xs_o[...] = xs
    bs_o[...] = bs
    cs_o[...] = conv_head(rim[:, CH + STATE :], c[...], tap_c[...])
    wide = dot(toward[...], head_rows(0, CH), precision=HIGHEST)
    row = lax.broadcasted_iota(jnp.int32, (16, 1), 0)
    feed = jnp.where(row < 8, xs.astype(F32) * wide, 0.0).astype(BF16)
    first = one[...] + dot(feed, bs, ((0,), (0,)))
    first_o[...] = first
    end0 = run0[7:8]
    end1 = run1[7:8]
    state = jnp.exp(head_columns(0, CH, end1)) * first + two[...]
    pay_o[:, 0:PIECE, :] = state.astype(BF16).reshape(PARTS, PIECE, STATE)
    total = head_columns(0, CH, end0 + end1).reshape(PARTS, PIECE, 1)[:, 0 : PAY - PIECE, :]
    total = jnp.broadcast_to(total, (PARTS, PAY - PIECE, STATE))
    high = total.astype(BF16).astype(F32)
    rest = total - high
    middle = rest.astype(BF16).astype(F32)
    low = rest - middle
    row = lax.broadcasted_iota(jnp.int32, total.shape, 1)
    pay_o[:, PIECE:PAY, :] = jnp.where(row == 0, high, jnp.where(row == 1, middle, low)).astype(BF16)


def prefix(got, out):
    log_total = got[:, PIECE : PIECE + 8, :].astype(F32)
    grow = jnp.exp(log_total[:, 0:1] + log_total[:, 1:2] + log_total[:, 2:3])
    state = jnp.zeros((PIECE, STATE), F32)
    for k in range(PARTS):
        out[k] = state.astype(BF16)
        if k < PARTS - 1:
            state = grow[k] * state + got[k, 0:PIECE, :].astype(F32)


def inside(xs, bs, cs, run, decay_t, step_t, skip, z, y_o, grow_o, scores, run_t):
    tile = pl.program_id(0)

    @pl.when(tile == 0)
    def _():
        later = lax.broadcasted_iota(jnp.int32, (SPAN, SPAN), 0)
        earlier = lax.broadcasted_iota(jnp.int32, (SPAN, SPAN), 1)
        upper = (later <= earlier).astype(F32)
        for k in range(2):
            rows = slice(k * SPAN, (k + 1) * SPAN)
            raw = dot(cs[rows], bs[rows], ((1,), (1,)))
            scores[rows] = jnp.where(later >= earlier, raw, 0.0)
            run_t[:, rows] = dot(decay_t[:, rows], upper, precision=HIGHEST)

    per_tile = TILE // HEAD_DIM
    head_lane = lax.broadcasted_iota(jnp.int32, (HEADS_LOCAL, 1), 0)
    lane_head = lax.broadcasted_iota(jnp.int32, (TOK, HEADS_LOCAL), 1)
    for q in range(per_tile):
        head = tile * per_tile + q
        column = jnp.sum(jnp.where(lane_head == head, run[...], 0.0), axis=1, keepdims=True)
        r_row = jnp.sum(jnp.where(head_lane == head, run_t[...], 0.0), axis=0, keepdims=True)
        s_row = jnp.sum(jnp.where(head_lane == head, step_t[...], 0.0), axis=0, keepdims=True)
        lanes = slice(q * HEAD_DIM, (q + 1) * HEAD_DIM)
        for k in range(2):
            rows = slice(k * SPAN, (k + 1) * SPAN)
            spread = jnp.minimum(column[rows] - r_row[:, rows], 0.0)
            weights = (jnp.exp(spread) * scores[rows] * s_row[:, rows]).astype(BF16)
            y_o[rows, lanes] = dot(weights, xs[rows, lanes])
    gate = jax.nn.silu(z[...].astype(F32))
    y_o[...] = (y_o[...] + skip[...] * xs[...].astype(F32)) * gate
    grow_o[...] = dot(jnp.exp(run[...]), head_rows(tile * per_tile, TILE), precision=HIGHEST) * gate


def rolled(distance):
    first = (distance + BEFORE) % 8 * SHARE
    return slice(first, first + SHARE)


def norm_project(y, grow, cs, run, first, incoming, gain, weight, *refs):
    outs, (normed, held, y_s, grow_s, sems) = refs[:-5], refs[-5:]
    half = outs[0].shape[1]
    steps = TOK // ROWS
    copies = []
    for step in range(steps):
        rows = slice(step * ROWS, (step + 1) * ROWS)
        copies.append(pltpu.make_async_copy(y.at[rows], y_s.at[rows], sems.at[2 * step]))
        copies.append(pltpu.make_async_copy(grow.at[rows], grow_s.at[rows], sems.at[2 * step + 1]))
    for group in range(2):
        lanes = slice(group * half, (group + 1) * half)
        copies.append(pltpu.make_async_copy(weight.at[:, lanes], held.at[:, lanes], sems.at[2 * steps + group]))
    for copy in copies:
        copy.start()
    place = lax.axis_index("tp")
    start = incoming[...]
    for step in range(steps):
        if step == SPAN // ROWS:
            decay = jnp.exp(head_columns(0, CH, run[SPAN - 1 : SPAN]))
            start = (decay * incoming[...].astype(F32) + first[...]).astype(BF16)
        rows = slice(step * ROWS, (step + 1) * ROWS)
        carried = dot(cs[rows], start, ((1,), (1,)))
        copies[2 * step].wait()
        copies[2 * step + 1].wait()
        gated = y_s[rows] + grow_s[rows] * carried
        meansq = jnp.sum(gated * gated, axis=1, keepdims=True) * (1.0 / CH)
        result = (gated * lax.rsqrt(meansq + 1e-05) * gain[...]).astype(BF16)
        for k in range(ROWS // SHARE):
            at = lax.rem(step * (ROWS // SHARE) + k - place + 8 + BEFORE, 8) * SHARE
            normed[pl.ds(pl.multiple_of(at, SHARE), SHARE)] = result[k * SHARE : (k + 1) * SHARE]
    for group in range(2):
        copies[2 * steps + group].wait()
        targets = [(outs[8 * group], 4 - group), (outs[8 * group + 1], -3 - group)]
        targets += [(outs[8 * group + 2 + k], k - 2 - group) for k in range(6)]
        for j in range(half // 512):
            lanes = slice(group * half + j * 512, group * half + (j + 1) * 512)
            sums = dot(normed[...], held[:, lanes])
            for out, distance in targets:
                out[:, j * 512 : (j + 1) * 512] = sums[rolled(distance)].astype(out.dtype)


def add_last(came, came_end, part, own, out, total):
    out[...] = (came[...].astype(F32) + part[...]).astype(BF16)
    total[...] = own[...] + came_end[...].astype(F32)


def add_two(came_up, came_down, part_up, part_down, up_o, down_o):
    up_o[...] = (came_up[...].astype(F32) + part_up[...]).astype(BF16)
    down_o[...] = (came_down[...].astype(F32) + part_down[...]).astype(BF16)


def finish(total_a, total_b, came_a, came_b, scale, out):
    row = lax.broadcasted_iota(jnp.int32, (HAD_BLOCK, HAD_BLOCK), 0)
    column = lax.broadcasted_iota(jnp.int32, (HAD_BLOCK, HAD_BLOCK), 1)
    ones = row & column
    ones = ones ^ (ones >> 4)
    ones = ones ^ (ones >> 2)
    ones = ones ^ (ones >> 1)
    table = (1 - 2 * (ones & 1)).astype(F32).astype(BF16)
    half = came_a.shape[1]
    for group, (total, came) in enumerate(((total_a, came_a), (total_b, came_b))):
        at = slice(group * half, (group + 1) * half)
        total = (total[...] + came[...].astype(F32)) * scale[:, at]
        stacked = jnp.concatenate(
            [total[:, k * HAD_BLOCK : (k + 1) * HAD_BLOCK] for k in range(half // HAD_BLOCK)], 0
        )
        high = stacked.astype(BF16)
        rest = stacked - high.astype(F32)
        middle = rest.astype(BF16)
        low = (rest - middle.astype(F32)).astype(BF16)
        rotated = dot(high, table) + dot(middle, table) + dot(low, table)
        rotated = (rotated * (1.0 / math.sqrt(HAD_BLOCK))).astype(BF16)
        for k in range(half // HAD_BLOCK):
            lanes = slice(group * half + k * HAD_BLOCK, group * half + (k + 1) * HAD_BLOCK)
            out[:, lanes] = rotated[k * SHARE : (k + 1) * SHARE]


def whole(shape):
    return pl.BlockSpec(shape, lambda i: (0,) * len(shape))


def tiled(shape, axis):
    return pl.BlockSpec(shape, lambda i: tuple(i if d == axis else 0 for d in range(len(shape))))


def params(mib):
    return pltpu.CompilerParams(vmem_limit_bytes=mib * MIB)


def ring(value, step):
    count = lax.axis_size("tp")
    return lax.ppermute(value, "tp", [(k, (k + step) % count) for k in range(count)])


def shape(dims, dtype):
    return jax.ShapeDtypeStruct(dims, dtype)


def block(dims, *index):
    return pl.BlockSpec(dims, lambda i: index)


def local(x_in, b_in, c_in, z_in, step_size, log_decay, conv_x, conv_b, conv_c, d_skip, norm_gain,
          out_weight, out_exponent, out_sign):
    seq = lax.axis_size("seq")
    tiles = CH // TILE
    step_t = step_size.T
    decay_t = log_decay.T
    last = TOK // 16 - 1
    tail = pl.pallas_call(
        tail_rows,
        grid=(1,),
        in_specs=[block((16, CH), last, 0), block((16, STATE), last, 0), block((16, STATE), last, 0)],
        out_specs=whole((16, CH + 2 * STATE)),
        out_shape=shape((16, CH + 2 * STATE), BF16),
        compiler_params=params(LIMIT["tail_rows"]),
        name="tail_rows",
    )(x_in, b_in, c_in)
    rim = lax.ppermute(tail, "seq", [(k, k + 1) for k in range(seq - 1)])
    xs, bs, cs, run, toward, one, two = pl.pallas_call(
        scan_in,
        grid=(tiles,),
        in_specs=[
            tiled((TOK, TILE), 1),
            whole((TOK, STATE)),
            whole((TOK, STATE)),
            whole((HEADS_LOCAL, TOK)),
            whole((HEADS_LOCAL, TOK)),
            tiled((4, TILE), 1),
            whole((4, STATE)),
            whole((4, STATE)),
        ],
        out_specs=[
            tiled((TOK, TILE), 1),
            whole((TOK, STATE)),
            whole((TOK, STATE)),
            whole((TOK, HEADS_LOCAL)),
            whole((TOK, HEADS_LOCAL)),
            tiled((TILE, STATE), 0),
            tiled((TILE, STATE), 0),
        ],
        out_shape=[
            shape((TOK, CH), BF16),
            shape((TOK, STATE), BF16),
            shape((TOK, STATE), BF16),
            shape((TOK, HEADS_LOCAL), F32),
            shape((TOK, HEADS_LOCAL), F32),
            shape((CH, STATE), F32),
            shape((CH, STATE), F32),
        ],
        scratch_shapes=[pltpu.VMEM((TOK + 8, TILE), F32)],
        compiler_params=params(LIMIT["scan_in"]),
        cost_estimate=pl.CostEstimate(flops=10**9, bytes_accessed=4 * 10**6, transcendentals=10**6),
        name="scan_in",
    )(x_in, b_in, c_in, step_t, decay_t, conv_x, conv_b, conv_c)

    xs, bs, cs, first, pay = pl.pallas_call(
        scan_edge,
        grid=(1,),
        in_specs=[
            whole((16, CH + 2 * STATE)),
            whole((16, CH)),
            whole((16, STATE)),
            whole((16, STATE)),
            whole((4, CH)),
            whole((4, STATE)),
            whole((4, STATE)),
            whole((16, HEADS_LOCAL)),
            block((8, HEADS_LOCAL), SPAN // 8 - 1, 0),
            block((8, HEADS_LOCAL), TOK // 8 - 1, 0),
            whole((CH, STATE)),
            whole((CH, STATE)),
            pl.BlockSpec(memory_space=pl.ANY),
            pl.BlockSpec(memory_space=pl.ANY),
            pl.BlockSpec(memory_space=pl.ANY),
        ],
        out_specs=[
            whole((16, CH)),
            whole((16, STATE)),
            whole((16, STATE)),
            whole((CH, STATE)),
            whole((PARTS, PAY, STATE)),
        ],
        out_shape=[
            shape((TOK, CH), BF16),
            shape((TOK, STATE), BF16),
            shape((TOK, STATE), BF16),
            shape((CH, STATE), F32),
            shape((PARTS, PAY, STATE), BF16),
        ],
        input_output_aliases={12: 0, 13: 1, 14: 2},
        compiler_params=params(LIMIT["scan_edge"]),
        name="scan_edge",
    )(rim, x_in, b_in, c_in, conv_x, conv_b, conv_c, toward, run, run, one, two, xs, bs, cs)

    got = lax.all_to_all(pay, "seq", 0, 0, tiled=True)
    y, grow = pl.pallas_call(
        inside,
        grid=(tiles,),
        in_specs=[
            tiled((TOK, TILE), 1),
            whole((TOK, STATE)),
            whole((TOK, STATE)),
            whole((TOK, HEADS_LOCAL)),
            whole((HEADS_LOCAL, TOK)),
            whole((HEADS_LOCAL, TOK)),
            tiled((1, TILE), 1),
            tiled((TOK, TILE), 1),
        ],
        out_specs=[tiled((TOK, TILE), 1), tiled((TOK, TILE), 1)],
        out_shape=[shape((TOK, CH), F32), shape((TOK, CH), F32)],
        scratch_shapes=[pltpu.VMEM((TOK, SPAN), F32), pltpu.VMEM((HEADS_LOCAL, TOK), F32)],
        compiler_params=params(LIMIT["inside"]),
        cost_estimate=pl.CostEstimate(flops=4 * 10**9, bytes_accessed=6 * 10**6, transcendentals=2 * 10**6),
        name="inside",
    )(xs, bs, cs, run, decay_t, step_t, jnp.repeat(d_skip, HEAD_DIM)[None, :], z_in)

    got, y, grow = lax.optimization_barrier((got, y, grow))
    before = pl.pallas_call(
        prefix,
        grid=(1,),
        in_specs=[whole((PARTS, PAY, STATE))],
        out_specs=whole((PARTS, PIECE, STATE)),
        out_shape=shape((PARTS, PIECE, STATE), BF16),
        compiler_params=params(LIMIT["prefix"]),
        name="prefix",
    )(got)
    incoming = lax.all_to_all(before, "seq", 0, 0, tiled=True).reshape(CH, STATE)

    model = out_weight.shape[1]
    half = model // 2
    vmem = pl.BlockSpec(memory_space=pltpu.VMEM)
    anywhere = pl.BlockSpec(memory_space=pl.ANY)
    outs = ([shape((SHARE, half), BF16)] * 2 + [shape((SHARE, half), PART)] * 6) * 2
    sums = pl.pallas_call(
        norm_project,
        in_specs=[anywhere] * 2 + [vmem] * 5 + [anywhere],
        out_specs=[vmem] * 16,
        out_shape=outs,
        scratch_shapes=[
            pltpu.VMEM((TOK, CH), BF16),
            pltpu.VMEM((CH, model), BF16),
            pltpu.VMEM((TOK, CH), F32),
            pltpu.VMEM((TOK, CH), F32),
            pltpu.SemaphoreType.DMA((2 * (TOK // ROWS) + 2,)),
        ],
        compiler_params=params(LIMIT["norm_project"]),
        cost_estimate=pl.CostEstimate(flops=10**9, bytes_accessed=10**7, transcendentals=0),
        name="norm_project",
    )(y, grow, cs, run, first, incoming, norm_gain[None, :], out_weight)
    up_a, down_a = sums[0:2]
    up_b, down_b = sums[8:10]
    parts = [sums[2:8], sums[10:16]]
    scale = jnp.exp2(out_exponent.astype(F32)) * out_sign.astype(F32)

    sent = shape((SHARE, half), BF16)

    def add(kernel, second, *operands):
        return pl.pallas_call(
            kernel,
            in_specs=[vmem] * 4,
            out_specs=[vmem] * 2,
            out_shape=[sent, second],
            compiler_params=params(LIMIT["ring"]),
            cost_estimate=pl.CostEstimate(flops=10**6, bytes_accessed=10**6, transcendentals=0),
            name=kernel.__name__,
        )(*operands)

    ends = []
    for group, (up, down) in enumerate(((up_a, down_a), (up_b, down_b))):
        lowest = (-2, -3)[group]
        mine = {distance: parts[group][distance - lowest] for distance in range(lowest, lowest + 6)}
        for hop in range(2):
            up, down = ring(up, 1), ring(down, -1)
            far = 3 - hop if group == 0 else 2 - hop
            up, down = add(add_two, sent, up, down, mine[far], mine[-(5 - far - 2 * hop)])
        up, down = ring(up, 1), ring(down, -1)
        sign = 1 if group == 0 else -1
        came, came_end = (up, down) if group == 0 else (down, up)
        value, total = add(add_last, shape((SHARE, half), F32), came, came_end, mine[sign], mine[0])
        ends += [total, ring(value, sign)]
    return pl.pallas_call(
        finish,
        in_specs=[vmem] * 5,
        out_specs=vmem,
        out_shape=shape((SHARE, model), BF16),
        compiler_params=params(LIMIT["ring"]),
        name="finish",
    )(ends[0], ends[2], ends[1], ends[3], scale[None, :])


def solution(mesh):
    return jax.shard_map(
        local,
        mesh=mesh,
        in_specs=(
            P("seq", "tp"),
            P("seq", "tp"),
            P("seq", "tp"),
            P("seq", "tp"),
            P("seq", "tp"),
            P("seq", "tp"),
            P(None, "tp"),
            P(None, "tp"),
            P(None, "tp"),
            P("tp"),
            P("tp"),
            P("tp", None),
            P(),
            P(),
        ),
        out_specs=P(("seq", "tp"), None),
        check_vma=False,
    )
```

```python
import functools
import math

import jax
import jax.numpy as jnp
from jax import lax
from jax.experimental import pallas as pl
from jax.experimental.pallas import tpu as pltpu
from jax.sharding import PartitionSpec as P

HEAD_DIM = 64
STATE = 128
SPAN = 256
HAD_BLOCK = 128
HEADS_LOCAL = 16
TOK = 512
CH = 1024
PARTS = 32
PIECE = 32
PAY = 48
TILE = 256
SCAN_TILE = 512
ROWS = 128
SHARE = 64
BEFORE = 3
MIB = 1024 * 1024
LIMIT = dict(tail_rows=58, scan_in=58, scan_edge=58, inside=58, prefix=16, norm_project=44, ring=24)

F32 = jnp.float32
BF16 = jnp.bfloat16
HIGHEST = lax.Precision.HIGHEST


def dot(a, b, dims=((1,), (0,)), precision=None):
    return lax.dot_general(a, b, (dims, ((), ())), precision=precision, preferred_element_type=F32)


def split(value, axis):
    high = value.astype(BF16)
    rest = value - high.astype(F32)
    middle = rest.astype(BF16)
    low = (rest - middle.astype(F32)).astype(BF16)
    return jnp.concatenate([high.astype(F32), middle.astype(F32), low.astype(F32)], axis).astype(BF16)


def expand(parts, first, channels):
    pattern = head_rows(first, channels)
    return dot(parts, jnp.concatenate([pattern] * 3, 0).astype(BF16))


def per_token(table, value_t):
    parts = dot(table, split(value_t, 0), ((1,), (1,)))
    h = HEADS_LOCAL
    return parts[:, 0:h] + parts[:, h : 2 * h] + parts[:, 2 * h : 3 * h]


def conv_silu(pad, rim, values, taps):
    width = values.shape[1]
    pad[0:8, 0:width] = rim[8:16].astype(F32)
    pad[8 : TOK + 8, 0:width] = values.astype(F32)
    total = taps[0:1] * pad[5 : 5 + TOK, 0:width]
    for k in range(1, 4):
        total = total + taps[k : k + 1] * pad[5 + k : 5 + k + TOK, 0:width]
    return jax.nn.silu(total).astype(BF16)


def head_rows(first, channels):
    head = lax.broadcasted_iota(jnp.int32, (HEADS_LOCAL, channels), 0)
    channel = lax.broadcasted_iota(jnp.int32, (HEADS_LOCAL, channels), 1)
    return (channel // HEAD_DIM + first == head).astype(F32)


def head_columns(first, channels, row):
    channel = lax.broadcasted_iota(jnp.int32, (channels, HEADS_LOCAL), 0)
    head = lax.broadcasted_iota(jnp.int32, (channels, HEADS_LOCAL), 1)
    return jnp.sum(jnp.where(channel // HEAD_DIM + first == head, row, 0.0), axis=1, keepdims=True)


def tail_rows(x, b, c, out):
    out[:, 0:CH] = x[...]
    out[:, CH : CH + STATE] = b[...]
    out[:, CH + STATE :] = c[...]


def scan_in(x, b, c, step_t, decay_t, tap_x, tap_b, tap_c, xs_o, bs_o, cs_o, run_o, toward_o, one_o, two_o, pad, parts):
    tile = pl.program_id(0)

    @pl.when(tile == 0)
    def _():
        empty = jnp.zeros((16, STATE), BF16)
        bs_o[...] = conv_silu(pad, empty, b[...], tap_b[...])
        cs_o[...] = conv_silu(pad, empty, c[...], tap_c[...])
        later = lax.broadcasted_iota(jnp.int32, (SPAN, SPAN), 0)
        earlier = lax.broadcasted_iota(jnp.int32, (SPAN, SPAN), 1)
        lower = (later >= earlier).astype(F32).astype(BF16)
        same = (later == earlier).astype(F32).astype(BF16)
        for k in range(2):
            rows = slice(k * SPAN, (k + 1) * SPAN)
            running = per_token(lower, decay_t[:, rows])
            step = per_token(same, step_t[:, rows])
            run_o[rows] = running
            toward = jnp.exp(running[SPAN - 1 :] - running) * step
            toward_o[rows] = toward
            parts[rows] = split(toward, 1)

    xs = conv_silu(pad, jnp.zeros((16, x.shape[1]), BF16), x[...], tap_x[...])
    xs_o[...] = xs
    wide = expand(parts[...], tile * (xs.shape[1] // HEAD_DIM), xs.shape[1])
    row = lax.broadcasted_iota(jnp.int32, (TOK, 1), 0)
    feed = jnp.where(row < 8, 0.0, xs.astype(F32) * wide).astype(BF16)
    one_o[...] = dot(feed[:SPAN], bs_o[:SPAN], ((0,), (0,)))
    two_o[...] = dot(feed[SPAN:], bs_o[SPAN:], ((0,), (0,)))


def conv_head(rim, values, taps):
    padded = jnp.concatenate([rim.astype(F32), values.astype(F32)], 0)
    total = taps[0:1] * padded[13:29]
    for k in range(1, 4):
        total = total + taps[k : k + 1] * padded[13 + k : 29 + k]
    return jax.nn.silu(total).astype(BF16)


def scan_edge(rim, x, b, c, tap_x, tap_b, tap_c, toward, run0, run1, one, two, xs_in, bs_in, cs_in,
              xs_o, bs_o, cs_o, first_o, pay_o):
    xs = conv_head(rim[:, 0:CH], x[...], tap_x[...])
    bs = conv_head(rim[:, CH : CH + STATE], b[...], tap_b[...])
    xs_o[...] = xs
    bs_o[...] = bs
    cs_o[...] = conv_head(rim[:, CH + STATE :], c[...], tap_c[...])
    wide = expand(split(toward[...], 1), 0, CH)
    row = lax.broadcasted_iota(jnp.int32, (16, 1), 0)
    feed = jnp.where(row < 8, xs.astype(F32) * wide, 0.0).astype(BF16)
    first = one[...] + dot(feed, bs, ((0,), (0,)))
    first_o[...] = first
    end0 = run0[7:8]
    end1 = run1[7:8]
    state = jnp.exp(head_columns(0, CH, end1)) * first + two[...]
    pay_o[:, 0:PIECE, :] = state.astype(BF16).reshape(PARTS, PIECE, STATE)
    total = head_columns(0, CH, end0 + end1).reshape(PARTS, PIECE, 1)[:, 0 : PAY - PIECE, :]
    total = jnp.broadcast_to(total, (PARTS, PAY - PIECE, STATE))
    high = total.astype(BF16).astype(F32)
    rest = total - high
    middle = rest.astype(BF16).astype(F32)
    low = rest - middle
    row = lax.broadcasted_iota(jnp.int32, total.shape, 1)
    pay_o[:, PIECE:PAY, :] = jnp.where(row == 0, high, jnp.where(row == 1, middle, low)).astype(BF16)


def prefix(got, out):
    log_total = got[:, PIECE : PIECE + 8, :].astype(F32)
    grow = jnp.exp(log_total[:, 0:1] + log_total[:, 1:2] + log_total[:, 2:3])
    state = jnp.zeros((PIECE, STATE), F32)
    for k in range(PARTS):
        out[k] = state.astype(BF16)
        if k < PARTS - 1:
            state = grow[k] * state + got[k, 0:PIECE, :].astype(F32)


def inside(xs, bs, cs, run, decay_t, step_t, skip, z, y_o, grow_o, scores, run_t, grown):
    tile = pl.program_id(0)

    @pl.when(tile == 0)
    def _():
        later = lax.broadcasted_iota(jnp.int32, (SPAN, SPAN), 0)
        earlier = lax.broadcasted_iota(jnp.int32, (SPAN, SPAN), 1)
        upper = (later <= earlier).astype(F32).astype(BF16)
        for k in range(2):
            rows = slice(k * SPAN, (k + 1) * SPAN)
            grown[rows] = split(jnp.exp(run[rows]), 1)
            raw = dot(cs[rows], bs[rows], ((1,), (1,)))
            scores[rows] = jnp.where(later >= earlier, raw, 0.0)
            parts = dot(split(decay_t[:, rows], 0), upper)
            run_t[:, rows] = parts[0:16] + parts[16:32] + parts[32:48]

    per_tile = TILE // HEAD_DIM
    head_lane = lax.broadcasted_iota(jnp.int32, (HEADS_LOCAL, 1), 0)
    lane_head = lax.broadcasted_iota(jnp.int32, (TOK, HEADS_LOCAL), 1)
    for q in range(per_tile):
        head = tile * per_tile + q
        column = jnp.sum(jnp.where(lane_head == head, run[...], 0.0), axis=1, keepdims=True)
        r_row = jnp.sum(jnp.where(head_lane == head, run_t[...], 0.0), axis=0, keepdims=True)
        s_row = jnp.sum(jnp.where(head_lane == head, step_t[...], 0.0), axis=0, keepdims=True)
        lanes = slice(q * HEAD_DIM, (q + 1) * HEAD_DIM)
        for k in range(2):
            rows = slice(k * SPAN, (k + 1) * SPAN)
            spread = jnp.minimum(column[rows] - r_row[:, rows], 0.0)
            weights = (jnp.exp(spread) * scores[rows] * s_row[:, rows]).astype(BF16)
            y_o[rows, lanes] = dot(weights, xs[rows, lanes])
    gate = jax.nn.silu(z[...].astype(F32))
    y_o[...] = (y_o[...] + skip[...] * xs[...].astype(F32)) * gate
    grow_o[...] = expand(grown[...], tile * per_tile, TILE) * gate


def rolled(distance):
    first = (distance + BEFORE) % 8 * SHARE
    return slice(first, first + SHARE)


def norm_project(y, grow, cs, run, first, incoming, gain, weight, *refs):
    outs, (normed, held, y_s, grow_s, sems) = refs[:-5], refs[-5:]
    half = 2 * outs[0].shape[1]
    steps = TOK // ROWS
    copies = []
    for step in range(steps):
        rows = slice(step * ROWS, (step + 1) * ROWS)
        copies.append(pltpu.make_async_copy(y.at[rows], y_s.at[rows], sems.at[2 * step]))
        copies.append(pltpu.make_async_copy(grow.at[rows], grow_s.at[rows], sems.at[2 * step + 1]))
    for group in range(2):
        lanes = slice(group * half, (group + 1) * half)
        copies.append(pltpu.make_async_copy(weight.at[:, lanes], held.at[:, lanes], sems.at[2 * steps + group]))
    for copy in copies:
        copy.start()
    place = lax.axis_index("tp")
    start = incoming[...]
    for step in range(steps):
        if step == SPAN // ROWS:
            decay = jnp.exp(head_columns(0, CH, run[SPAN - 1 : SPAN]))
            start = (decay * incoming[...].astype(F32) + first[...]).astype(BF16)
        rows = slice(step * ROWS, (step + 1) * ROWS)
        carried = dot(cs[rows], start, ((1,), (1,)))
        copies[2 * step].wait()
        copies[2 * step + 1].wait()
        gated = y_s[rows] + grow_s[rows] * carried
        meansq = jnp.sum(gated * gated, axis=1, keepdims=True) * (1.0 / CH)
        result = (gated * lax.rsqrt(meansq + 1e-05) * gain[...]).astype(BF16)
        for k in range(ROWS // SHARE):
            at = lax.rem(step * (ROWS // SHARE) + k - place + 8 + BEFORE, 8) * SHARE
            normed[pl.ds(pl.multiple_of(at, SHARE), SHARE)] = result[k * SHARE : (k + 1) * SHARE]
    for group in range(2):
        copies[2 * steps + group].wait()
        mine = outs[9 * group : 9 * group + 9]
        for j in range(half // 512):
            lanes = slice(group * half + j * 512, group * half + (j + 1) * 512)
            sums = dot(normed[...], held[:, lanes])
            far = mine[2 * j * 512 // half]
            inner = j * 512 % (half // 2)
            far[:, inner : inner + 512] = sums[rolled(4)].astype(BF16)
            for k in range(7):
                mine[2 + k][:, j * 512 : (j + 1) * 512] = sums[rolled(k - 3)]


def add_far(came_up, came_down, part_up, part_down, up_o, down_o):
    part = came_up.shape[1]
    up_o[:, :part] = (came_up[...].astype(F32) + part_up[:, :part]).astype(BF16)
    up_o[:, part:] = part_up[:, part:].astype(BF16)
    down_o[:, :part] = part_down[:, :part].astype(BF16)
    down_o[:, part:] = (came_down[...].astype(F32) + part_down[:, part:]).astype(BF16)


def add_two(came_up, came_down, part_up, part_down, up_o, down_o):
    up_o[...] = (came_up[...].astype(F32) + part_up[...]).astype(BF16)
    down_o[...] = (came_down[...].astype(F32) + part_down[...]).astype(BF16)


def finish(own_a, up_a, down_a, own_b, up_b, down_b, scale, out):
    row = lax.broadcasted_iota(jnp.int32, (HAD_BLOCK, HAD_BLOCK), 0)
    column = lax.broadcasted_iota(jnp.int32, (HAD_BLOCK, HAD_BLOCK), 1)
    ones = row & column
    ones = ones ^ (ones >> 4)
    ones = ones ^ (ones >> 2)
    ones = ones ^ (ones >> 1)
    table = (1 - 2 * (ones & 1)).astype(F32).astype(BF16)
    half = up_a.shape[1]
    for group, (own, up, down) in enumerate(((own_a, up_a, down_a), (own_b, up_b, down_b))):
        at = slice(group * half, (group + 1) * half)
        total = (own[...] + up[...].astype(F32) + down[...].astype(F32)) * scale[:, at]
        stacked = jnp.concatenate(
            [total[:, k * HAD_BLOCK : (k + 1) * HAD_BLOCK] for k in range(half // HAD_BLOCK)], 0
        )
        high = stacked.astype(BF16)
        rest = stacked - high.astype(F32)
        middle = rest.astype(BF16)
        low = (rest - middle.astype(F32)).astype(BF16)
        rotated = dot(high, table) + dot(middle, table) + dot(low, table)
        rotated = (rotated * (1.0 / math.sqrt(HAD_BLOCK))).astype(BF16)
        for k in range(half // HAD_BLOCK):
            lanes = slice(group * half + k * HAD_BLOCK, group * half + (k + 1) * HAD_BLOCK)
            out[:, lanes] = rotated[k * SHARE : (k + 1) * SHARE]


def whole(shape):
    return pl.BlockSpec(shape, lambda i: (0,) * len(shape))


def tiled(shape, axis):
    return pl.BlockSpec(shape, lambda i: tuple(i if d == axis else 0 for d in range(len(shape))))


def params(mib):
    return pltpu.CompilerParams(vmem_limit_bytes=mib * MIB)


def ring(value, step):
    count = lax.axis_size("tp")
    return lax.ppermute(value, "tp", [(k, (k + step) % count) for k in range(count)])


def shape(dims, dtype):
    return jax.ShapeDtypeStruct(dims, dtype)


def block(dims, *index):
    return pl.BlockSpec(dims, lambda i: index)


def local(x_in, b_in, c_in, z_in, step_size, log_decay, conv_x, conv_b, conv_c, d_skip, norm_gain,
          out_weight, out_exponent, out_sign):
    seq = lax.axis_size("seq")
    tiles = CH // TILE
    step_t = step_size.T
    decay_t = log_decay.T
    last = TOK // 16 - 1
    tail = pl.pallas_call(
        tail_rows,
        grid=(1,),
        in_specs=[block((16, CH), last, 0), block((16, STATE), last, 0), block((16, STATE), last, 0)],
        out_specs=whole((16, CH + 2 * STATE)),
        out_shape=shape((16, CH + 2 * STATE), BF16),
        compiler_params=params(LIMIT["tail_rows"]),
        name="tail_rows",
    )(x_in, b_in, c_in)
    rim = lax.ppermute(tail, "seq", [(k, k + 1) for k in range(seq - 1)])
    xs, bs, cs, run, toward, one, two = pl.pallas_call(
        scan_in,
        grid=(CH // SCAN_TILE,),
        in_specs=[
            tiled((TOK, SCAN_TILE), 1),
            whole((TOK, STATE)),
            whole((TOK, STATE)),
            whole((HEADS_LOCAL, TOK)),
            whole((HEADS_LOCAL, TOK)),
            tiled((4, SCAN_TILE), 1),
            whole((4, STATE)),
            whole((4, STATE)),
        ],
        out_specs=[
            tiled((TOK, SCAN_TILE), 1),
            whole((TOK, STATE)),
            whole((TOK, STATE)),
            whole((TOK, HEADS_LOCAL)),
            whole((TOK, HEADS_LOCAL)),
            tiled((SCAN_TILE, STATE), 0),
            tiled((SCAN_TILE, STATE), 0),
        ],
        out_shape=[
            shape((TOK, CH), BF16),
            shape((TOK, STATE), BF16),
            shape((TOK, STATE), BF16),
            shape((TOK, HEADS_LOCAL), F32),
            shape((TOK, HEADS_LOCAL), F32),
            shape((CH, STATE), F32),
            shape((CH, STATE), F32),
        ],
        scratch_shapes=[pltpu.VMEM((TOK + 8, SCAN_TILE), F32), pltpu.VMEM((TOK, 3 * HEADS_LOCAL), BF16)],
        compiler_params=params(LIMIT["scan_in"]),
        cost_estimate=pl.CostEstimate(flops=10**9, bytes_accessed=4 * 10**6, transcendentals=10**6),
        name="scan_in",
    )(x_in, b_in, c_in, step_t, decay_t, conv_x, conv_b, conv_c)

    xs, bs, cs, first, pay = pl.pallas_call(
        scan_edge,
        grid=(1,),
        in_specs=[
            whole((16, CH + 2 * STATE)),
            whole((16, CH)),
            whole((16, STATE)),
            whole((16, STATE)),
            whole((4, CH)),
            whole((4, STATE)),
            whole((4, STATE)),
            whole((16, HEADS_LOCAL)),
            block((8, HEADS_LOCAL), SPAN // 8 - 1, 0),
            block((8, HEADS_LOCAL), TOK // 8 - 1, 0),
            whole((CH, STATE)),
            whole((CH, STATE)),
            pl.BlockSpec(memory_space=pl.ANY),
            pl.BlockSpec(memory_space=pl.ANY),
            pl.BlockSpec(memory_space=pl.ANY),
        ],
        out_specs=[
            whole((16, CH)),
            whole((16, STATE)),
            whole((16, STATE)),
            whole((CH, STATE)),
            whole((PARTS, PAY, STATE)),
        ],
        out_shape=[
            shape((TOK, CH), BF16),
            shape((TOK, STATE), BF16),
            shape((TOK, STATE), BF16),
            shape((CH, STATE), F32),
            shape((PARTS, PAY, STATE), BF16),
        ],
        input_output_aliases={12: 0, 13: 1, 14: 2},
        compiler_params=params(LIMIT["scan_edge"]),
        name="scan_edge",
    )(rim, x_in, b_in, c_in, conv_x, conv_b, conv_c, toward, run, run, one, two, xs, bs, cs)

    got = lax.all_to_all(pay, "seq", 0, 0, tiled=True)
    y, grow = pl.pallas_call(
        inside,
        grid=(tiles,),
        in_specs=[
            tiled((TOK, TILE), 1),
            whole((TOK, STATE)),
            whole((TOK, STATE)),
            whole((TOK, HEADS_LOCAL)),
            whole((HEADS_LOCAL, TOK)),
            whole((HEADS_LOCAL, TOK)),
            tiled((1, TILE), 1),
            tiled((TOK, TILE), 1),
        ],
        out_specs=[tiled((TOK, TILE), 1), tiled((TOK, TILE), 1)],
        out_shape=[shape((TOK, CH), F32), shape((TOK, CH), F32)],
        scratch_shapes=[
            pltpu.VMEM((TOK, SPAN), F32),
            pltpu.VMEM((HEADS_LOCAL, TOK), F32),
            pltpu.VMEM((TOK, 3 * HEADS_LOCAL), BF16),
        ],
        compiler_params=params(LIMIT["inside"]),
        cost_estimate=pl.CostEstimate(flops=4 * 10**9, bytes_accessed=6 * 10**6, transcendentals=2 * 10**6),
        name="inside",
    )(xs, bs, cs, run, decay_t, step_t, jnp.repeat(d_skip, HEAD_DIM)[None, :], z_in)


    before = pl.pallas_call(
        prefix,
        grid=(1,),
        in_specs=[whole((PARTS, PAY, STATE))],
        out_specs=whole((PARTS, PIECE, STATE)),
        out_shape=shape((PARTS, PIECE, STATE), BF16),
        compiler_params=params(LIMIT["prefix"]),
        name="prefix",
    )(got)
    incoming = lax.all_to_all(before, "seq", 0, 0, tiled=True).reshape(CH, STATE)

    model = out_weight.shape[1]
    half = model // 2
    vmem = pl.BlockSpec(memory_space=pltpu.VMEM)
    anywhere = pl.BlockSpec(memory_space=pl.ANY)
    outs = ([shape((SHARE, half // 2), BF16)] * 2 + [shape((SHARE, half), F32)] * 7) * 2
    sums = pl.pallas_call(
        norm_project,
        in_specs=[anywhere] * 2 + [vmem] * 5 + [anywhere],
        out_specs=[vmem] * 18,
        out_shape=outs,
        scratch_shapes=[
            pltpu.VMEM((TOK, CH), BF16),
            pltpu.VMEM((CH, model), BF16),
            pltpu.VMEM((TOK, CH), F32),
            pltpu.VMEM((TOK, CH), F32),
            pltpu.SemaphoreType.DMA((2 * (TOK // ROWS) + 2,)),
        ],
        compiler_params=params(LIMIT["norm_project"]),
        cost_estimate=pl.CostEstimate(flops=10**9, bytes_accessed=10**7, transcendentals=0),
        name="norm_project",
    )(y, grow, cs, run, first, incoming, norm_gain[None, :], out_weight)
    scale = jnp.exp2(out_exponent.astype(F32)) * out_sign.astype(F32)

    sent = shape((SHARE, half), BF16)

    def add(kernel, *operands):
        return pl.pallas_call(
            kernel,
            in_specs=[vmem] * 4,
            out_specs=[vmem] * 2,
            out_shape=[sent] * 2,
            compiler_params=params(LIMIT["ring"]),
            cost_estimate=pl.CostEstimate(flops=10**6, bytes_accessed=10**6, transcendentals=0),
            name=kernel.__name__,
        )(*operands)

    ends = []
    for group in range(2):
        up, down = sums[9 * group : 9 * group + 2]
        mine = {distance: sums[9 * group + 5 + distance] for distance in range(-3, 4)}
        for distance in (3, 2, 1):
            up, down = ring(up, 1), ring(down, -1)
            up, down = add(add_far if distance == 3 else add_two, up, down, mine[distance], mine[-distance])
        ends += [mine[0], ring(up, 1), ring(down, -1)]
    return pl.pallas_call(
        finish,
        in_specs=[vmem] * 7,
        out_specs=vmem,
        out_shape=shape((SHARE, model), BF16),
        compiler_params=params(LIMIT["ring"]),
        name="finish",
    )(*ends, scale[None, :])


def solution(mesh):
    return jax.shard_map(
        local,
        mesh=mesh,
        in_specs=(
            P("seq", "tp"),
            P("seq", "tp"),
            P("seq", "tp"),
            P("seq", "tp"),
            P("seq", "tp"),
            P("seq", "tp"),
            P(None, "tp"),
            P(None, "tp"),
            P(None, "tp"),
            P("tp"),
            P("tp"),
            P("tp", None),
            P(),
            P(),
        ),
        out_specs=P(("seq", "tp"), None),
        check_vma=False,
    )
```

```python
import functools
import math

import jax
import jax.numpy as jnp
from jax import lax
from jax.experimental import pallas as pl
from jax.experimental.pallas import tpu as pltpu
from jax.sharding import PartitionSpec as P

HEAD_DIM = 64
STATE = 128
SPAN = 256
HAD_BLOCK = 128
HEADS_LOCAL = 16
TOK = 512
CH = 1024
PARTS = 32
PIECE = 32
PAY = 48
TILE = 256
SCAN_TILE = 512
ROWS = 128
SHARE = 64
BEFORE = 3
MIB = 1024 * 1024
LIMIT = dict(tail_rows=58, scan_in=58, scan_edge=58, inside=58, prefix=16, norm_project=47, project=44, ring=24)

F32 = jnp.float32
BF16 = jnp.bfloat16
HIGHEST = lax.Precision.HIGHEST


def dot(a, b, dims=((1,), (0,)), precision=None):
    return lax.dot_general(a, b, (dims, ((), ())), precision=precision, preferred_element_type=F32)


def split(value, axis):
    high = value.astype(BF16)
    rest = value - high.astype(F32)
    middle = rest.astype(BF16)
    low = (rest - middle.astype(F32)).astype(BF16)
    return jnp.concatenate([high.astype(F32), middle.astype(F32), low.astype(F32)], axis).astype(BF16)


def expand(parts, first, channels):
    pattern = head_rows(first, channels)
    return dot(parts, jnp.concatenate([pattern] * 3, 0).astype(BF16))


def per_token(table, value_t):
    parts = dot(table, split(value_t, 0), ((1,), (1,)))
    h = HEADS_LOCAL
    return parts[:, 0:h] + parts[:, h : 2 * h] + parts[:, 2 * h : 3 * h]


def conv_silu(pad, rim, values, taps):
    width = values.shape[1]
    pad[0:8, 0:width] = rim[8:16].astype(F32)
    pad[8 : TOK + 8, 0:width] = values.astype(F32)
    total = taps[0:1] * pad[5 : 5 + TOK, 0:width]
    for k in range(1, 4):
        total = total + taps[k : k + 1] * pad[5 + k : 5 + k + TOK, 0:width]
    return jax.nn.silu(total).astype(BF16)


def head_rows(first, channels):
    head = lax.broadcasted_iota(jnp.int32, (HEADS_LOCAL, channels), 0)
    channel = lax.broadcasted_iota(jnp.int32, (HEADS_LOCAL, channels), 1)
    return (channel // HEAD_DIM + first == head).astype(F32)


def head_columns(first, channels, row):
    channel = lax.broadcasted_iota(jnp.int32, (channels, HEADS_LOCAL), 0)
    head = lax.broadcasted_iota(jnp.int32, (channels, HEADS_LOCAL), 1)
    return jnp.sum(jnp.where(channel // HEAD_DIM + first == head, row, 0.0), axis=1, keepdims=True)


def tail_rows(x, b, c, out):
    out[:, 0:CH] = x[...]
    out[:, CH : CH + STATE] = b[...]
    out[:, CH + STATE :] = c[...]


def scan_in(x, b, c, step_t, decay_t, tap_x, tap_b, tap_c, xs_o, bs_o, cs_o, run_o, toward_o, one_o, two_o, pad, parts):
    tile = pl.program_id(0)

    @pl.when(tile == 0)
    def _():
        empty = jnp.zeros((16, STATE), BF16)
        bs_o[...] = conv_silu(pad, empty, b[...], tap_b[...])
        cs_o[...] = conv_silu(pad, empty, c[...], tap_c[...])
        later = lax.broadcasted_iota(jnp.int32, (SPAN, SPAN), 0)
        earlier = lax.broadcasted_iota(jnp.int32, (SPAN, SPAN), 1)
        lower = (later >= earlier).astype(F32).astype(BF16)
        same = (later == earlier).astype(F32).astype(BF16)
        for k in range(2):
            rows = slice(k * SPAN, (k + 1) * SPAN)
            running = per_token(lower, decay_t[:, rows])
            step = per_token(same, step_t[:, rows])
            run_o[rows] = running
            toward = jnp.exp(running[SPAN - 1 :] - running) * step
            toward_o[rows] = toward
            parts[rows] = split(toward, 1)

    xs = conv_silu(pad, jnp.zeros((16, x.shape[1]), BF16), x[...], tap_x[...])
    xs_o[...] = xs
    wide = expand(parts[...], tile * (xs.shape[1] // HEAD_DIM), xs.shape[1])
    row = lax.broadcasted_iota(jnp.int32, (TOK, 1), 0)
    feed = jnp.where(row < 8, 0.0, xs.astype(F32) * wide).astype(BF16)
    one_o[...] = dot(feed[:SPAN], bs_o[:SPAN], ((0,), (0,)))
    two_o[...] = dot(feed[SPAN:], bs_o[SPAN:], ((0,), (0,)))


def conv_head(rim, values, taps):
    padded = jnp.concatenate([rim.astype(F32), values.astype(F32)], 0)
    total = taps[0:1] * padded[13:29]
    for k in range(1, 4):
        total = total + taps[k : k + 1] * padded[13 + k : 29 + k]
    return jax.nn.silu(total).astype(BF16)


def scan_edge(rim, x, b, c, tap_x, tap_b, tap_c, toward, run0, run1, one, two, xs_in, bs_in, cs_in,
              xs_o, bs_o, cs_o, first_o, pay_o):
    xs = conv_head(rim[:, 0:CH], x[...], tap_x[...])
    bs = conv_head(rim[:, CH : CH + STATE], b[...], tap_b[...])
    xs_o[...] = xs
    bs_o[...] = bs
    cs_o[...] = conv_head(rim[:, CH + STATE :], c[...], tap_c[...])
    wide = expand(split(toward[...], 1), 0, CH)
    row = lax.broadcasted_iota(jnp.int32, (16, 1), 0)
    feed = jnp.where(row < 8, xs.astype(F32) * wide, 0.0).astype(BF16)
    first = one[...] + dot(feed, bs, ((0,), (0,)))
    first_o[...] = first
    end0 = run0[7:8]
    end1 = run1[7:8]
    state = jnp.exp(head_columns(0, CH, end1)) * first + two[...]
    pay_o[:, 0:PIECE, :] = state.astype(BF16).reshape(PARTS, PIECE, STATE)
    total = head_columns(0, CH, end0 + end1).reshape(PARTS, PIECE, 1)[:, 0 : PAY - PIECE, :]
    total = jnp.broadcast_to(total, (PARTS, PAY - PIECE, STATE))
    high = total.astype(BF16).astype(F32)
    rest = total - high
    middle = rest.astype(BF16).astype(F32)
    low = rest - middle
    row = lax.broadcasted_iota(jnp.int32, total.shape, 1)
    pay_o[:, PIECE:PAY, :] = jnp.where(row == 0, high, jnp.where(row == 1, middle, low)).astype(BF16)


def prefix(got, out):
    log_total = got[:, PIECE : PIECE + 8, :].astype(F32)
    grow = jnp.exp(log_total[:, 0:1] + log_total[:, 1:2] + log_total[:, 2:3])
    state = jnp.zeros((PIECE, STATE), F32)
    for k in range(PARTS):
        out[k] = state.astype(BF16)
        if k < PARTS - 1:
            state = grow[k] * state + got[k, 0:PIECE, :].astype(F32)


def inside(xs, bs, cs, run, decay_t, step_t, skip, z, y_o, grow_o, scores, run_t, grown):
    tile = pl.program_id(0)

    @pl.when(tile == 0)
    def _():
        later = lax.broadcasted_iota(jnp.int32, (SPAN, SPAN), 0)
        earlier = lax.broadcasted_iota(jnp.int32, (SPAN, SPAN), 1)
        upper = (later <= earlier).astype(F32).astype(BF16)
        for k in range(2):
            rows = slice(k * SPAN, (k + 1) * SPAN)
            grown[rows] = split(jnp.exp(run[rows]), 1)
            raw = dot(cs[rows], bs[rows], ((1,), (1,)))
            scores[rows] = jnp.where(later >= earlier, raw, 0.0)
            parts = dot(split(decay_t[:, rows], 0), upper)
            run_t[:, rows] = parts[0:16] + parts[16:32] + parts[32:48]

    per_tile = TILE // HEAD_DIM
    head_lane = lax.broadcasted_iota(jnp.int32, (HEADS_LOCAL, 1), 0)
    lane_head = lax.broadcasted_iota(jnp.int32, (TOK, HEADS_LOCAL), 1)
    for q in range(per_tile):
        head = tile * per_tile + q
        column = jnp.sum(jnp.where(lane_head == head, run[...], 0.0), axis=1, keepdims=True)
        r_row = jnp.sum(jnp.where(head_lane == head, run_t[...], 0.0), axis=0, keepdims=True)
        s_row = jnp.sum(jnp.where(head_lane == head, step_t[...], 0.0), axis=0, keepdims=True)
        lanes = slice(q * HEAD_DIM, (q + 1) * HEAD_DIM)
        for k in range(2):
            rows = slice(k * SPAN, (k + 1) * SPAN)
            spread = jnp.minimum(column[rows] - r_row[:, rows], 0.0)
            weights = (jnp.exp(spread) * scores[rows] * s_row[:, rows]).astype(BF16)
            y_o[rows, lanes] = dot(weights, xs[rows, lanes])
    gate = jax.nn.silu(z[...].astype(F32))
    y_o[...] = (y_o[...] + skip[...] * xs[...].astype(F32)) * gate
    grow_o[...] = expand(grown[...], tile * per_tile, TILE) * gate


def rolled(distance):
    first = (distance + BEFORE) % 8 * SHARE
    return slice(first, first + SHARE)


def norm_project(y, grow, cs, run, first, incoming, gain, weight, normed, *refs):
    outs, (held, y_s, grow_s, sems) = refs[:-4], refs[-4:]
    half = 2 * outs[0].shape[1]
    steps = TOK // ROWS
    copies = []
    for step in range(steps):
        rows = slice(step * ROWS, (step + 1) * ROWS)
        copies.append(pltpu.make_async_copy(y.at[rows], y_s.at[rows], sems.at[2 * step]))
        copies.append(pltpu.make_async_copy(grow.at[rows], grow_s.at[rows], sems.at[2 * step + 1]))
    for group in range(2):
        lanes = slice(group * half, (group + 1) * half)
        copies.append(pltpu.make_async_copy(weight.at[:, lanes], held.at[:, lanes], sems.at[2 * steps + group]))
    for copy in copies:
        copy.start()
    place = lax.axis_index("tp")
    start = incoming[...]
    for step in range(steps):
        if step == SPAN // ROWS:
            decay = jnp.exp(head_columns(0, CH, run[SPAN - 1 : SPAN]))
            start = (decay * incoming[...].astype(F32) + first[...]).astype(BF16)
        rows = slice(step * ROWS, (step + 1) * ROWS)
        carried = dot(cs[rows], start, ((1,), (1,)))
        copies[2 * step].wait()
        copies[2 * step + 1].wait()
        gated = y_s[rows] + grow_s[rows] * carried
        meansq = jnp.sum(gated * gated, axis=1, keepdims=True) * (1.0 / CH)
        result = (gated * lax.rsqrt(meansq + 1e-05) * gain[...]).astype(BF16)
        for k in range(ROWS // SHARE):
            at = lax.rem(step * (ROWS // SHARE) + k - place + 8 + BEFORE, 8) * SHARE
            normed[pl.ds(pl.multiple_of(at, SHARE), SHARE)] = result[k * SHARE : (k + 1) * SHARE]
    for group in range(2):
        copies[2 * steps + group].wait()
        for j in range(half // 512):
            lanes = slice(group * half + j * 512, group * half + (j + 1) * 512)
            far = outs[2 * group + 2 * j * 512 // half]
            inner = j * 512 % (half // 2)
            if group == 1:
                far[:, inner : inner + 512] = dot(normed[rolled(4)], held[:, lanes]).astype(BF16)
                continue
            sums = dot(normed[...], held[:, lanes])
            far[:, inner : inner + 512] = sums[rolled(4)].astype(BF16)
            for k in range(7):
                outs[4 + k][:, j * 512 : (j + 1) * 512] = sums[rolled(k - 3)]


def project(group, normed, weight, *refs):
    outs, (held, sems) = refs[:-2], refs[-2:]
    half = outs[0].shape[1]
    copies = []
    for j in range(half // 512):
        here = slice(j * 512, (j + 1) * 512)
        there = slice(group * half + j * 512, group * half + (j + 1) * 512)
        copies.append(pltpu.make_async_copy(weight.at[:, there], held.at[:, here], sems.at[j]))
    for copy in copies:
        copy.start()
    for j, copy in enumerate(copies):
        here = slice(j * 512, (j + 1) * 512)
        copy.wait()
        sums = dot(normed[0 : 7 * SHARE], held[:, here])
        for k in range(7):
            outs[k][:, here] = sums[k * SHARE : (k + 1) * SHARE]


def add_far(came_up, came_down, part_up, part_down, up_o, down_o):
    part = came_up.shape[1]
    up_o[:, :part] = (came_up[...].astype(F32) + part_up[:, :part]).astype(BF16)
    up_o[:, part:] = part_up[:, part:].astype(BF16)
    down_o[:, :part] = part_down[:, :part].astype(BF16)
    down_o[:, part:] = (came_down[...].astype(F32) + part_down[:, part:]).astype(BF16)


def add_two(came_up, came_down, part_up, part_down, up_o, down_o):
    up_o[...] = (came_up[...].astype(F32) + part_up[...]).astype(BF16)
    down_o[...] = (came_down[...].astype(F32) + part_down[...]).astype(BF16)


def finish(own_a, up_a, down_a, own_b, up_b, down_b, scale, out):
    row = lax.broadcasted_iota(jnp.int32, (HAD_BLOCK, HAD_BLOCK), 0)
    column = lax.broadcasted_iota(jnp.int32, (HAD_BLOCK, HAD_BLOCK), 1)
    ones = row & column
    ones = ones ^ (ones >> 4)
    ones = ones ^ (ones >> 2)
    ones = ones ^ (ones >> 1)
    table = (1 - 2 * (ones & 1)).astype(F32).astype(BF16)
    half = up_a.shape[1]
    for group, (own, up, down) in enumerate(((own_a, up_a, down_a), (own_b, up_b, down_b))):
        at = slice(group * half, (group + 1) * half)
        total = (own[...] + up[...].astype(F32) + down[...].astype(F32)) * scale[:, at]
        stacked = jnp.concatenate(
            [total[:, k * HAD_BLOCK : (k + 1) * HAD_BLOCK] for k in range(half // HAD_BLOCK)], 0
        )
        high = stacked.astype(BF16)
        rest = stacked - high.astype(F32)
        middle = rest.astype(BF16)
        low = (rest - middle.astype(F32)).astype(BF16)
        rotated = dot(high, table) + dot(middle, table) + dot(low, table)
        rotated = (rotated * (1.0 / math.sqrt(HAD_BLOCK))).astype(BF16)
        for k in range(half // HAD_BLOCK):
            lanes = slice(group * half + k * HAD_BLOCK, group * half + (k + 1) * HAD_BLOCK)
            out[:, lanes] = rotated[k * SHARE : (k + 1) * SHARE]


def whole(shape):
    return pl.BlockSpec(shape, lambda i: (0,) * len(shape))


def tiled(shape, axis):
    return pl.BlockSpec(shape, lambda i: tuple(i if d == axis else 0 for d in range(len(shape))))


def params(mib):
    return pltpu.CompilerParams(vmem_limit_bytes=mib * MIB)


def ring(value, step):
    count = lax.axis_size("tp")
    return lax.ppermute(value, "tp", [(k, (k + step) % count) for k in range(count)])


def shape(dims, dtype):
    return jax.ShapeDtypeStruct(dims, dtype)


def block(dims, *index):
    return pl.BlockSpec(dims, lambda i: index)


def local(x_in, b_in, c_in, z_in, step_size, log_decay, conv_x, conv_b, conv_c, d_skip, norm_gain,
          out_weight, out_exponent, out_sign):
    seq = lax.axis_size("seq")
    tiles = CH // TILE
    step_t = step_size.T
    decay_t = log_decay.T
    last = TOK // 16 - 1
    tail = pl.pallas_call(
        tail_rows,
        grid=(1,),
        in_specs=[block((16, CH), last, 0), block((16, STATE), last, 0), block((16, STATE), last, 0)],
        out_specs=whole((16, CH + 2 * STATE)),
        out_shape=shape((16, CH + 2 * STATE), BF16),
        compiler_params=params(LIMIT["tail_rows"]),
        name="tail_rows",
    )(x_in, b_in, c_in)
    rim = lax.ppermute(tail, "seq", [(k, k + 1) for k in range(seq - 1)])
    xs, bs, cs, run, toward, one, two = pl.pallas_call(
        scan_in,
        grid=(CH // SCAN_TILE,),
        in_specs=[
            tiled((TOK, SCAN_TILE), 1),
            whole((TOK, STATE)),
            whole((TOK, STATE)),
            whole((HEADS_LOCAL, TOK)),
            whole((HEADS_LOCAL, TOK)),
            tiled((4, SCAN_TILE), 1),
            whole((4, STATE)),
            whole((4, STATE)),
        ],
        out_specs=[
            tiled((TOK, SCAN_TILE), 1),
            whole((TOK, STATE)),
            whole((TOK, STATE)),
            whole((TOK, HEADS_LOCAL)),
            whole((TOK, HEADS_LOCAL)),
            tiled((SCAN_TILE, STATE), 0),
            tiled((SCAN_TILE, STATE), 0),
        ],
        out_shape=[
            shape((TOK, CH), BF16),
            shape((TOK, STATE), BF16),
            shape((TOK, STATE), BF16),
            shape((TOK, HEADS_LOCAL), F32),
            shape((TOK, HEADS_LOCAL), F32),
            shape((CH, STATE), F32),
            shape((CH, STATE), F32),
        ],
        scratch_shapes=[pltpu.VMEM((TOK + 8, SCAN_TILE), F32), pltpu.VMEM((TOK, 3 * HEADS_LOCAL), BF16)],
        compiler_params=params(LIMIT["scan_in"]),
        cost_estimate=pl.CostEstimate(flops=10**9, bytes_accessed=4 * 10**6, transcendentals=10**6),
        name="scan_in",
    )(x_in, b_in, c_in, step_t, decay_t, conv_x, conv_b, conv_c)

    xs, bs, cs, first, pay = pl.pallas_call(
        scan_edge,
        grid=(1,),
        in_specs=[
            whole((16, CH + 2 * STATE)),
            whole((16, CH)),
            whole((16, STATE)),
            whole((16, STATE)),
            whole((4, CH)),
            whole((4, STATE)),
            whole((4, STATE)),
            whole((16, HEADS_LOCAL)),
            block((8, HEADS_LOCAL), SPAN // 8 - 1, 0),
            block((8, HEADS_LOCAL), TOK // 8 - 1, 0),
            whole((CH, STATE)),
            whole((CH, STATE)),
            pl.BlockSpec(memory_space=pl.ANY),
            pl.BlockSpec(memory_space=pl.ANY),
            pl.BlockSpec(memory_space=pl.ANY),
        ],
        out_specs=[
            whole((16, CH)),
            whole((16, STATE)),
            whole((16, STATE)),
            whole((CH, STATE)),
            whole((PARTS, PAY, STATE)),
        ],
        out_shape=[
            shape((TOK, CH), BF16),
            shape((TOK, STATE), BF16),
            shape((TOK, STATE), BF16),
            shape((CH, STATE), F32),
            shape((PARTS, PAY, STATE), BF16),
        ],
        input_output_aliases={12: 0, 13: 1, 14: 2},
        compiler_params=params(LIMIT["scan_edge"]),
        name="scan_edge",
    )(rim, x_in, b_in, c_in, conv_x, conv_b, conv_c, toward, run, run, one, two, xs, bs, cs)

    got = lax.all_to_all(pay, "seq", 0, 0, tiled=True)
    y, grow = pl.pallas_call(
        inside,
        grid=(tiles,),
        in_specs=[
            tiled((TOK, TILE), 1),
            whole((TOK, STATE)),
            whole((TOK, STATE)),
            whole((TOK, HEADS_LOCAL)),
            whole((HEADS_LOCAL, TOK)),
            whole((HEADS_LOCAL, TOK)),
            tiled((1, TILE), 1),
            tiled((TOK, TILE), 1),
        ],
        out_specs=[tiled((TOK, TILE), 1), tiled((TOK, TILE), 1)],
        out_shape=[shape((TOK, CH), F32), shape((TOK, CH), F32)],
        scratch_shapes=[
            pltpu.VMEM((TOK, SPAN), F32),
            pltpu.VMEM((HEADS_LOCAL, TOK), F32),
            pltpu.VMEM((TOK, 3 * HEADS_LOCAL), BF16),
        ],
        compiler_params=params(LIMIT["inside"]),
        cost_estimate=pl.CostEstimate(flops=4 * 10**9, bytes_accessed=6 * 10**6, transcendentals=2 * 10**6),
        name="inside",
    )(xs, bs, cs, run, decay_t, step_t, jnp.repeat(d_skip, HEAD_DIM)[None, :], z_in)


    before = pl.pallas_call(
        prefix,
        grid=(1,),
        in_specs=[whole((PARTS, PAY, STATE))],
        out_specs=whole((PARTS, PIECE, STATE)),
        out_shape=shape((PARTS, PIECE, STATE), BF16),
        compiler_params=params(LIMIT["prefix"]),
        name="prefix",
    )(got)
    incoming = lax.all_to_all(before, "seq", 0, 0, tiled=True).reshape(CH, STATE)

    model = out_weight.shape[1]
    half = model // 2
    vmem = pl.BlockSpec(memory_space=pltpu.VMEM)
    anywhere = pl.BlockSpec(memory_space=pl.ANY)
    normed, *sums = pl.pallas_call(
        norm_project,
        in_specs=[anywhere] * 2 + [vmem] * 5 + [anywhere],
        out_specs=[vmem] * 12,
        out_shape=[shape((TOK, CH), BF16)] + [shape((SHARE, half // 2), BF16)] * 4 + [shape((SHARE, half), F32)] * 7,
        scratch_shapes=[
            pltpu.VMEM((CH, model), BF16),
            pltpu.VMEM((TOK, CH), F32),
            pltpu.VMEM((TOK, CH), F32),
            pltpu.SemaphoreType.DMA((2 * (TOK // ROWS) + 2,)),
        ],
        compiler_params=params(LIMIT["norm_project"]),
        cost_estimate=pl.CostEstimate(flops=10**9, bytes_accessed=10**7, transcendentals=0),
        name="norm_project",
    )(y, grow, cs, run, first, incoming, norm_gain[None, :], out_weight)
    fars = sums[0:4]
    rest = pl.pallas_call(
        functools.partial(project, 1),
        in_specs=[vmem, anywhere],
        out_specs=[vmem] * 7,
        out_shape=[shape((SHARE, half), F32)] * 7,
        scratch_shapes=[pltpu.VMEM((CH, half), BF16), pltpu.SemaphoreType.DMA((half // 512,))],
        compiler_params=params(LIMIT["project"]),
        cost_estimate=pl.CostEstimate(flops=10, bytes_accessed=10, transcendentals=0),
        name="project",
    )(normed, out_weight)
    parts = [sums[4:11], rest]
    scale = jnp.exp2(out_exponent.astype(F32)) * out_sign.astype(F32)

    sent = shape((SHARE, half), BF16)

    def add(kernel, *operands):
        return pl.pallas_call(
            kernel,
            in_specs=[vmem] * 4,
            out_specs=[vmem] * 2,
            out_shape=[sent] * 2,
            compiler_params=params(LIMIT["ring"]),
            cost_estimate=pl.CostEstimate(flops=10**6, bytes_accessed=10**6, transcendentals=0),
            name=kernel.__name__,
        )(*operands)

    ends = []
    for group in range(2):
        up, down = fars[2 * group : 2 * group + 2]
        mine = {distance: parts[group][3 + distance] for distance in range(-3, 4)}
        for distance in (3, 2, 1):
            up, down = ring(up, 1), ring(down, -1)
            up, down = add(add_far if distance == 3 else add_two, up, down, mine[distance], mine[-distance])
        ends += [mine[0], ring(up, 1), ring(down, -1)]
    return pl.pallas_call(
        finish,
        in_specs=[vmem] * 7,
        out_specs=vmem,
        out_shape=shape((SHARE, model), BF16),
        compiler_params=params(LIMIT["ring"]),
        name="finish",
    )(*ends, scale[None, :])


def solution(mesh):
    return jax.shard_map(
        local,
        mesh=mesh,
        in_specs=(
            P("seq", "tp"),
            P("seq", "tp"),
            P("seq", "tp"),
            P("seq", "tp"),
            P("seq", "tp"),
            P("seq", "tp"),
            P(None, "tp"),
            P(None, "tp"),
            P(None, "tp"),
            P("tp"),
            P("tp"),
            P("tp", None),
            P(),
            P(),
        ),
        out_specs=P(("seq", "tp"), None),
        check_vma=False,
    )
```

```python
import functools
import math

import jax
import jax.numpy as jnp
from jax import lax
from jax.experimental import pallas as pl
from jax.experimental.pallas import tpu as pltpu
from jax.sharding import PartitionSpec as P

HEAD_DIM = 64
STATE = 128
SPAN = 256
HAD_BLOCK = 128
HEADS_LOCAL = 16
TOK = 512
CH = 1024
PARTS = 32
PIECE = 32
PAY = 48
TILE = 256
SCAN_TILE = 512
ROWS = 128
SHARE = 64
BEFORE = 3
MIB = 1024 * 1024
LIMIT = dict(tail_rows=58, scan_in=58, scan_edge=58, inside=58, prefix=16, norm_project=47, project=44, ring=24)

F32 = jnp.float32
BF16 = jnp.bfloat16
HIGHEST = lax.Precision.HIGHEST


def dot(a, b, dims=((1,), (0,)), precision=None):
    return lax.dot_general(a, b, (dims, ((), ())), precision=precision, preferred_element_type=F32)


def split(value, axis):
    high = value.astype(BF16)
    rest = value - high.astype(F32)
    middle = rest.astype(BF16)
    low = (rest - middle.astype(F32)).astype(BF16)
    return jnp.concatenate([high.astype(F32), middle.astype(F32), low.astype(F32)], axis).astype(BF16)


def expand(parts, first, channels):
    pattern = head_rows(first, channels)
    return dot(parts, jnp.concatenate([pattern] * 3, 0).astype(BF16))


def per_token(table, value_t):
    parts = dot(table, split(value_t, 0), ((1,), (1,)))
    h = HEADS_LOCAL
    return parts[:, 0:h] + parts[:, h : 2 * h] + parts[:, 2 * h : 3 * h]


def conv_silu(pad, rim, values, taps):
    width = values.shape[1]
    pad[0:8, 0:width] = rim[8:16].astype(F32)
    pad[8 : TOK + 8, 0:width] = values.astype(F32)
    total = taps[0:1] * pad[5 : 5 + TOK, 0:width]
    for k in range(1, 4):
        total = total + taps[k : k + 1] * pad[5 + k : 5 + k + TOK, 0:width]
    return jax.nn.silu(total).astype(BF16)


def head_rows(first, channels):
    head = lax.broadcasted_iota(jnp.int32, (HEADS_LOCAL, channels), 0)
    channel = lax.broadcasted_iota(jnp.int32, (HEADS_LOCAL, channels), 1)
    return (channel // HEAD_DIM + first == head).astype(F32)


def head_columns(first, channels, row):
    channel = lax.broadcasted_iota(jnp.int32, (channels, HEADS_LOCAL), 0)
    head = lax.broadcasted_iota(jnp.int32, (channels, HEADS_LOCAL), 1)
    return jnp.sum(jnp.where(channel // HEAD_DIM + first == head, row, 0.0), axis=1, keepdims=True)


def tail_rows(x, b, c, out):
    out[:, 0:CH] = x[...]
    out[:, CH : CH + STATE] = b[...]
    out[:, CH + STATE :] = c[...]


def head_spread(row):
    a = lax.broadcasted_iota(jnp.int32, (HEADS_LOCAL, HEADS_LOCAL), 0)
    b = lax.broadcasted_iota(jnp.int32, (HEADS_LOCAL, HEADS_LOCAL), 1)
    column = jnp.sum(jnp.where(a == b, row, 0.0), axis=1, keepdims=True)
    channel = lax.broadcasted_iota(jnp.int32, (CH, 3 * HEADS_LOCAL), 0)
    head = lax.broadcasted_iota(jnp.int32, (CH, 3 * HEADS_LOCAL), 1)
    pattern = (channel // HEAD_DIM == head % HEADS_LOCAL).astype(F32).astype(BF16)
    return dot(pattern, split(jnp.broadcast_to(column, (HEADS_LOCAL, STATE)), 0))


def scan_in(x, b, c, step_t, decay_t, tap_x, tap_b, tap_c, xs_o, bs_o, cs_o, run_o, toward_o, one_o, two_o, pad, parts):
    tile = pl.program_id(0)

    @pl.when(tile == 0)
    def _():
        empty = jnp.zeros((16, STATE), BF16)
        bs_o[...] = conv_silu(pad, empty, b[...], tap_b[...])
        cs_o[...] = conv_silu(pad, empty, c[...], tap_c[...])
        later = lax.broadcasted_iota(jnp.int32, (SPAN, SPAN), 0)
        earlier = lax.broadcasted_iota(jnp.int32, (SPAN, SPAN), 1)
        lower = (later >= earlier).astype(F32).astype(BF16)
        same = (later == earlier).astype(F32).astype(BF16)
        for k in range(2):
            rows = slice(k * SPAN, (k + 1) * SPAN)
            running = per_token(lower, decay_t[:, rows])
            step = per_token(same, step_t[:, rows])
            run_o[rows] = running
            toward = jnp.exp(running[SPAN - 1 :] - running) * step
            toward_o[rows] = toward
            parts[rows] = split(toward, 1)

    xs = conv_silu(pad, jnp.zeros((16, x.shape[1]), BF16), x[...], tap_x[...])
    xs_o[...] = xs
    wide = expand(parts[...], tile * (xs.shape[1] // HEAD_DIM), xs.shape[1])
    row = lax.broadcasted_iota(jnp.int32, (TOK, 1), 0)
    feed = jnp.where(row < 8, 0.0, xs.astype(F32) * wide).astype(BF16)
    one_o[...] = dot(feed[:SPAN], bs_o[:SPAN], ((0,), (0,)))
    two_o[...] = dot(feed[SPAN:], bs_o[SPAN:], ((0,), (0,)))


def conv_head(rim, values, taps):
    padded = jnp.concatenate([rim.astype(F32), values.astype(F32)], 0)
    total = taps[0:1] * padded[13:29]
    for k in range(1, 4):
        total = total + taps[k : k + 1] * padded[13 + k : 29 + k]
    return jax.nn.silu(total).astype(BF16)


def scan_edge(rim, x, b, c, tap_x, tap_b, tap_c, toward, run0, run1, one, two, xs_in, bs_in, cs_in,
              xs_o, bs_o, cs_o, first_o, pay_o):
    xs = conv_head(rim[:, 0:CH], x[...], tap_x[...])
    bs = conv_head(rim[:, CH : CH + STATE], b[...], tap_b[...])
    xs_o[...] = xs
    bs_o[...] = bs
    cs_o[...] = conv_head(rim[:, CH + STATE :], c[...], tap_c[...])
    wide = expand(split(toward[...], 1), 0, CH)
    row = lax.broadcasted_iota(jnp.int32, (16, 1), 0)
    feed = jnp.where(row < 8, xs.astype(F32) * wide, 0.0).astype(BF16)
    first = one[...] + dot(feed, bs, ((0,), (0,)))
    first_o[...] = first
    end0 = run0[7:8]
    end1 = run1[7:8]
    state = jnp.exp(head_spread(end1)) * first + two[...]
    pay_o[:, 0:PIECE, :] = state.astype(BF16).reshape(PARTS, PIECE, STATE)
    total = head_spread(end0 + end1).reshape(PARTS, PIECE, STATE)[:, 0 : PAY - PIECE, :]
    high = total.astype(BF16).astype(F32)
    rest = total - high
    middle = rest.astype(BF16).astype(F32)
    low = rest - middle
    row = lax.broadcasted_iota(jnp.int32, total.shape, 1)
    pay_o[:, PIECE:PAY, :] = jnp.where(row == 0, high, jnp.where(row == 1, middle, low)).astype(BF16)


def prefix(got, out):
    log_total = got[:, PIECE : PIECE + 8, :].astype(F32)
    grow = jnp.exp(log_total[:, 0:1] + log_total[:, 1:2] + log_total[:, 2:3])
    state = jnp.zeros((PIECE, STATE), F32)
    for k in range(PARTS):
        out[k] = state.astype(BF16)
        if k < PARTS - 1:
            state = grow[k] * state + got[k, 0:PIECE, :].astype(F32)


def inside(xs, bs, cs, run, decay_t, step_t, skip, z, y_o, grow_o, scores, run_t, grown):
    tile = pl.program_id(0)

    @pl.when(tile == 0)
    def _():
        later = lax.broadcasted_iota(jnp.int32, (SPAN, SPAN), 0)
        earlier = lax.broadcasted_iota(jnp.int32, (SPAN, SPAN), 1)
        upper = (later <= earlier).astype(F32).astype(BF16)
        for k in range(2):
            rows = slice(k * SPAN, (k + 1) * SPAN)
            grown[rows] = split(jnp.exp(run[rows]), 1)
            raw = dot(cs[rows], bs[rows], ((1,), (1,)))
            scores[rows] = jnp.where(later >= earlier, raw, 0.0)
            parts = dot(split(decay_t[:, rows], 0), upper)
            run_t[:, rows] = parts[0:16] + parts[16:32] + parts[32:48]

    per_tile = TILE // HEAD_DIM
    head_lane = lax.broadcasted_iota(jnp.int32, (HEADS_LOCAL, 1), 0)
    lane_head = lax.broadcasted_iota(jnp.int32, (TOK, HEADS_LOCAL), 1)
    for q in range(per_tile):
        head = tile * per_tile + q
        column = jnp.sum(jnp.where(lane_head == head, run[...], 0.0), axis=1, keepdims=True)
        r_row = jnp.sum(jnp.where(head_lane == head, run_t[...], 0.0), axis=0, keepdims=True)
        s_row = jnp.sum(jnp.where(head_lane == head, step_t[...], 0.0), axis=0, keepdims=True)
        lanes = slice(q * HEAD_DIM, (q + 1) * HEAD_DIM)
        for k in range(2):
            rows = slice(k * SPAN, (k + 1) * SPAN)
            spread = jnp.minimum(column[rows] - r_row[:, rows], 0.0)
            weights = (jnp.exp(spread) * scores[rows] * s_row[:, rows]).astype(BF16)
            y_o[rows, lanes] = dot(weights, xs[rows, lanes])
    gate = jax.nn.silu(z[...].astype(F32))
    y_o[...] = (y_o[...] + skip[...] * xs[...].astype(F32)) * gate
    grow_o[...] = expand(grown[...], tile * per_tile, TILE) * gate


def rolled(distance):
    first = (distance + BEFORE) % 8 * SHARE
    return slice(first, first + SHARE)


def norm_project(y, grow, cs, run, first, incoming, gain, weight, normed, *refs):
    outs, (held, y_s, grow_s, sems) = refs[:-4], refs[-4:]
    half = 2 * outs[0].shape[1]
    steps = TOK // ROWS
    copies = []
    for step in range(steps):
        rows = slice(step * ROWS, (step + 1) * ROWS)
        copies.append(pltpu.make_async_copy(y.at[rows], y_s.at[rows], sems.at[2 * step]))
        copies.append(pltpu.make_async_copy(grow.at[rows], grow_s.at[rows], sems.at[2 * step + 1]))
    for group in range(2):
        lanes = slice(group * half, (group + 1) * half)
        copies.append(pltpu.make_async_copy(weight.at[:, lanes], held.at[:, lanes], sems.at[2 * steps + group]))
    for copy in copies:
        copy.start()
    place = lax.axis_index("tp")
    start = incoming[...]
    for step in range(steps):
        if step == SPAN // ROWS:
            decay = jnp.exp(head_spread(run[SPAN - 1 : SPAN]))
            start = (decay * incoming[...].astype(F32) + first[...]).astype(BF16)
        rows = slice(step * ROWS, (step + 1) * ROWS)
        carried = dot(cs[rows], start, ((1,), (1,)))
        copies[2 * step].wait()
        copies[2 * step + 1].wait()
        gated = y_s[rows] + grow_s[rows] * carried
        meansq = jnp.sum(gated * gated, axis=1, keepdims=True) * (1.0 / CH)
        result = (gated * lax.rsqrt(meansq + 1e-05) * gain[...]).astype(BF16)
        for k in range(ROWS // SHARE):
            at = lax.rem(step * (ROWS // SHARE) + k - place + 8 + BEFORE, 8) * SHARE
            normed[pl.ds(pl.multiple_of(at, SHARE), SHARE)] = result[k * SHARE : (k + 1) * SHARE]
    for group in range(2):
        copies[2 * steps + group].wait()
        for j in range(half // 512):
            lanes = slice(group * half + j * 512, group * half + (j + 1) * 512)
            far = outs[2 * group + 2 * j * 512 // half]
            inner = j * 512 % (half // 2)
            if group == 1:
                far[:, inner : inner + 512] = dot(normed[rolled(4)], held[:, lanes]).astype(BF16)
                continue
            sums = dot(normed[...], held[:, lanes])
            far[:, inner : inner + 512] = sums[rolled(4)].astype(BF16)
            for k in range(7):
                outs[4 + k][:, j * 512 : (j + 1) * 512] = sums[rolled(k - 3)]


def project(group, normed, weight, *refs):
    outs, (held, sems) = refs[:-2], refs[-2:]
    half = outs[0].shape[1]
    copies = []
    for j in range(half // 512):
        here = slice(j * 512, (j + 1) * 512)
        there = slice(group * half + j * 512, group * half + (j + 1) * 512)
        copies.append(pltpu.make_async_copy(weight.at[:, there], held.at[:, here], sems.at[j]))
    for copy in copies:
        copy.start()
    for j, copy in enumerate(copies):
        here = slice(j * 512, (j + 1) * 512)
        copy.wait()
        sums = dot(normed[0 : 7 * SHARE], held[:, here])
        for k in range(7):
            outs[k][:, here] = sums[k * SHARE : (k + 1) * SHARE]


def add_far(came_up, came_down, part_up, part_down, up_o, down_o):
    part = came_up.shape[1]
    up_o[:, :part] = (came_up[...].astype(F32) + part_up[:, :part]).astype(BF16)
    up_o[:, part:] = part_up[:, part:].astype(BF16)
    down_o[:, :part] = part_down[:, :part].astype(BF16)
    down_o[:, part:] = (came_down[...].astype(F32) + part_down[:, part:]).astype(BF16)


def add_two(came_up, came_down, part_up, part_down, up_o, down_o):
    up_o[...] = (came_up[...].astype(F32) + part_up[...]).astype(BF16)
    down_o[...] = (came_down[...].astype(F32) + part_down[...]).astype(BF16)


def finish(group, own, up, down, scale, *refs):
    out = refs[-1]
    row = lax.broadcasted_iota(jnp.int32, (HAD_BLOCK, HAD_BLOCK), 0)
    column = lax.broadcasted_iota(jnp.int32, (HAD_BLOCK, HAD_BLOCK), 1)
    ones = row & column
    ones = ones ^ (ones >> 4)
    ones = ones ^ (ones >> 2)
    ones = ones ^ (ones >> 1)
    table = (1 - 2 * (ones & 1)).astype(F32).astype(BF16)
    half = up.shape[1]
    at = slice(group * half, (group + 1) * half)
    total = (own[...] + up[...].astype(F32) + down[...].astype(F32)) * scale[:, at]
    stacked = jnp.concatenate([total[:, k * HAD_BLOCK : (k + 1) * HAD_BLOCK] for k in range(half // HAD_BLOCK)], 0)
    high = stacked.astype(BF16)
    rest = stacked - high.astype(F32)
    middle = rest.astype(BF16)
    low = (rest - middle.astype(F32)).astype(BF16)
    rotated = dot(high, table) + dot(middle, table) + dot(low, table)
    rotated = (rotated * (1.0 / math.sqrt(HAD_BLOCK))).astype(BF16)
    for k in range(half // HAD_BLOCK):
        out[:, k * HAD_BLOCK : (k + 1) * HAD_BLOCK] = rotated[k * SHARE : (k + 1) * SHARE]


def whole(shape):
    return pl.BlockSpec(shape, lambda i: (0,) * len(shape))


def tiled(shape, axis):
    return pl.BlockSpec(shape, lambda i: tuple(i if d == axis else 0 for d in range(len(shape))))


def params(mib):
    return pltpu.CompilerParams(vmem_limit_bytes=mib * MIB)


def ring(value, step):
    count = lax.axis_size("tp")
    return lax.ppermute(value, "tp", [(k, (k + step) % count) for k in range(count)])


def shape(dims, dtype):
    return jax.ShapeDtypeStruct(dims, dtype)


def block(dims, *index):
    return pl.BlockSpec(dims, lambda i: index)


def local(x_in, b_in, c_in, z_in, step_size, log_decay, conv_x, conv_b, conv_c, d_skip, norm_gain,
          out_weight, out_exponent, out_sign):
    seq = lax.axis_size("seq")
    tiles = CH // TILE
    step_t = step_size.T
    decay_t = log_decay.T
    last = TOK // 16 - 1
    tail = pl.pallas_call(
        tail_rows,
        grid=(1,),
        in_specs=[block((16, CH), last, 0), block((16, STATE), last, 0), block((16, STATE), last, 0)],
        out_specs=whole((16, CH + 2 * STATE)),
        out_shape=shape((16, CH + 2 * STATE), BF16),
        compiler_params=params(LIMIT["tail_rows"]),
        name="tail_rows",
    )(x_in, b_in, c_in)
    rim = lax.ppermute(tail, "seq", [(k, k + 1) for k in range(seq - 1)])
    xs, bs, cs, run, toward, one, two = pl.pallas_call(
        scan_in,
        grid=(CH // SCAN_TILE,),
        in_specs=[
            tiled((TOK, SCAN_TILE), 1),
            whole((TOK, STATE)),
            whole((TOK, STATE)),
            whole((HEADS_LOCAL, TOK)),
            whole((HEADS_LOCAL, TOK)),
            tiled((4, SCAN_TILE), 1),
            whole((4, STATE)),
            whole((4, STATE)),
        ],
        out_specs=[
            tiled((TOK, SCAN_TILE), 1),
            whole((TOK, STATE)),
            whole((TOK, STATE)),
            whole((TOK, HEADS_LOCAL)),
            whole((TOK, HEADS_LOCAL)),
            tiled((SCAN_TILE, STATE), 0),
            tiled((SCAN_TILE, STATE), 0),
        ],
        out_shape=[
            shape((TOK, CH), BF16),
            shape((TOK, STATE), BF16),
            shape((TOK, STATE), BF16),
            shape((TOK, HEADS_LOCAL), F32),
            shape((TOK, HEADS_LOCAL), F32),
            shape((CH, STATE), F32),
            shape((CH, STATE), F32),
        ],
        scratch_shapes=[pltpu.VMEM((TOK + 8, SCAN_TILE), F32), pltpu.VMEM((TOK, 3 * HEADS_LOCAL), BF16)],
        compiler_params=params(LIMIT["scan_in"]),
        cost_estimate=pl.CostEstimate(flops=10**9, bytes_accessed=4 * 10**6, transcendentals=10**6),
        name="scan_in",
    )(x_in, b_in, c_in, step_t, decay_t, conv_x, conv_b, conv_c)

    xs, bs, cs, first, pay = pl.pallas_call(
        scan_edge,
        grid=(1,),
        in_specs=[
            whole((16, CH + 2 * STATE)),
            whole((16, CH)),
            whole((16, STATE)),
            whole((16, STATE)),
            whole((4, CH)),
            whole((4, STATE)),
            whole((4, STATE)),
            whole((16, HEADS_LOCAL)),
            block((8, HEADS_LOCAL), SPAN // 8 - 1, 0),
            block((8, HEADS_LOCAL), TOK // 8 - 1, 0),
            whole((CH, STATE)),
            whole((CH, STATE)),
            pl.BlockSpec(memory_space=pl.ANY),
            pl.BlockSpec(memory_space=pl.ANY),
            pl.BlockSpec(memory_space=pl.ANY),
        ],
        out_specs=[
            whole((16, CH)),
            whole((16, STATE)),
            whole((16, STATE)),
            whole((CH, STATE)),
            whole((PARTS, PAY, STATE)),
        ],
        out_shape=[
            shape((TOK, CH), BF16),
            shape((TOK, STATE), BF16),
            shape((TOK, STATE), BF16),
            shape((CH, STATE), F32),
            shape((PARTS, PAY, STATE), BF16),
        ],
        input_output_aliases={12: 0, 13: 1, 14: 2},
        compiler_params=params(LIMIT["scan_edge"]),
        name="scan_edge",
    )(rim, x_in, b_in, c_in, conv_x, conv_b, conv_c, toward, run, run, one, two, xs, bs, cs)

    got = lax.all_to_all(pay, "seq", 0, 0, tiled=True)
    y, grow = pl.pallas_call(
        inside,
        grid=(tiles,),
        in_specs=[
            tiled((TOK, TILE), 1),
            whole((TOK, STATE)),
            whole((TOK, STATE)),
            whole((TOK, HEADS_LOCAL)),
            whole((HEADS_LOCAL, TOK)),
            whole((HEADS_LOCAL, TOK)),
            tiled((1, TILE), 1),
            tiled((TOK, TILE), 1),
        ],
        out_specs=[tiled((TOK, TILE), 1), tiled((TOK, TILE), 1)],
        out_shape=[shape((TOK, CH), F32), shape((TOK, CH), F32)],
        scratch_shapes=[
            pltpu.VMEM((TOK, SPAN), F32),
            pltpu.VMEM((HEADS_LOCAL, TOK), F32),
            pltpu.VMEM((TOK, 3 * HEADS_LOCAL), BF16),
        ],
        compiler_params=params(LIMIT["inside"]),
        cost_estimate=pl.CostEstimate(flops=4 * 10**9, bytes_accessed=6 * 10**6, transcendentals=2 * 10**6),
        name="inside",
    )(xs, bs, cs, run, decay_t, step_t, jnp.repeat(d_skip, HEAD_DIM)[None, :], z_in)


    before = pl.pallas_call(
        prefix,
        grid=(1,),
        in_specs=[whole((PARTS, PAY, STATE))],
        out_specs=whole((PARTS, PIECE, STATE)),
        out_shape=shape((PARTS, PIECE, STATE), BF16),
        compiler_params=params(LIMIT["prefix"]),
        name="prefix",
    )(got)
    incoming = lax.all_to_all(before, "seq", 0, 0, tiled=True).reshape(CH, STATE)

    model = out_weight.shape[1]
    half = model // 2
    vmem = pl.BlockSpec(memory_space=pltpu.VMEM)
    anywhere = pl.BlockSpec(memory_space=pl.ANY)
    normed, *sums = pl.pallas_call(
        norm_project,
        in_specs=[anywhere] * 2 + [vmem] * 5 + [anywhere],
        out_specs=[vmem] * 12,
        out_shape=[shape((TOK, CH), BF16)] + [shape((SHARE, half // 2), BF16)] * 4 + [shape((SHARE, half), F32)] * 7,
        scratch_shapes=[
            pltpu.VMEM((CH, model), BF16),
            pltpu.VMEM((TOK, CH), F32),
            pltpu.VMEM((TOK, CH), F32),
            pltpu.SemaphoreType.DMA((2 * (TOK // ROWS) + 2,)),
        ],
        compiler_params=params(LIMIT["norm_project"]),
        cost_estimate=pl.CostEstimate(flops=10**9, bytes_accessed=10**7, transcendentals=0),
        name="norm_project",
    )(y, grow, cs, run, first, incoming, norm_gain[None, :], out_weight)
    fars = sums[0:4]
    rest = pl.pallas_call(
        functools.partial(project, 1),
        in_specs=[vmem, anywhere],
        out_specs=[vmem] * 7,
        out_shape=[shape((SHARE, half), F32)] * 7,
        scratch_shapes=[pltpu.VMEM((CH, half), BF16), pltpu.SemaphoreType.DMA((half // 512,))],
        compiler_params=params(LIMIT["project"]),
        cost_estimate=pl.CostEstimate(flops=10, bytes_accessed=10, transcendentals=0),
        name="project",
    )(normed, out_weight)
    parts = [sums[4:11], rest]
    scale = jnp.exp2(out_exponent.astype(F32)) * out_sign.astype(F32)

    sent = shape((SHARE, half), BF16)

    def add(kernel, *operands):
        return pl.pallas_call(
            kernel,
            in_specs=[vmem] * 4,
            out_specs=[vmem] * 2,
            out_shape=[sent] * 2,
            compiler_params=params(LIMIT["ring"]),
            cost_estimate=pl.CostEstimate(flops=10**6, bytes_accessed=10**6, transcendentals=0),
            name=kernel.__name__,
        )(*operands)

    ends = []
    for group in range(2):
        up, down = fars[2 * group : 2 * group + 2]
        mine = {distance: parts[group][3 + distance] for distance in range(-3, 4)}
        for distance in (3, 2, 1):
            up, down = ring(up, 1), ring(down, -1)
            up, down = add(add_far if distance == 3 else add_two, up, down, mine[distance], mine[-distance])
        ends += [mine[0], ring(up, 1), ring(down, -1)]
    result = []
    for group in (1, 0):
        result = [
            pl.pallas_call(
                functools.partial(finish, group),
                grid=(1,),
                in_specs=[vmem] * 4 + [anywhere] * len(result),
                out_specs=block((SHARE, half), 0, group),
                out_shape=shape((SHARE, model), BF16),
                input_output_aliases={4: 0} if result else {},
                compiler_params=params(LIMIT["ring"]),
                name="finish",
            )(*ends[3 * group : 3 * group + 3], scale[None, :], *result)
        ]
    return result[0]


def solution(mesh):
    return jax.shard_map(
        local,
        mesh=mesh,
        in_specs=(
            P("seq", "tp"),
            P("seq", "tp"),
            P("seq", "tp"),
            P("seq", "tp"),
            P("seq", "tp"),
            P("seq", "tp"),
            P(None, "tp"),
            P(None, "tp"),
            P(None, "tp"),
            P("tp"),
            P("tp"),
            P("tp", None),
            P(),
            P(),
        ),
        out_specs=P(("seq", "tp"), None),
        check_vma=False,
    )
```
